128 devices in a mesh: sec: 16 (over z, x), az: 8 (over y, core).
Axes of the slice: x: 4, y: 4, z: 4, core: 2. Of those that a mesh axis runs over, the one named last changes fastest.
Arguments:
- currents: float32 [256, 16, 1024], P(('sec', 'az')), may hold values from -6 to 6
- right_side: float32 [256, 16, 1024], P(('sec', 'az')), may hold values from -6 to 6
- counts: int32 [256], P(('sec', 'az')), may hold values from 128 to 1024, as said below
- inverse_blocks: bfloat16 [256, 1024, 1024], P(('sec', 'az')), may hold values from -0.1875 to 0.1875
- near_out: bfloat16 [256, 4, 128, 1024], P(('sec', 'az')), may hold values from -0.1875 to 0.1875
- near_in: bfloat16 [256, 4, 128, 1024], P(('sec', 'az')), may hold values from -0.5 to 0.5
- far_source_basis: bfloat16 [256, 32, 1024], P(('sec', 'az')), may hold values from -0.1875 to 0.1875
- far_target_basis: bfloat16 [256, 32, 1024], P(('sec', 'az')), may hold values from -1 to 1
- far_cores: bfloat16 [196608, 1024], P(('sec', 'az')), may hold values from -0.0390625 to 0.0390625
- far_target_device: int32 [196608, 1], P(('sec', 'az')), may hold values from 0 to 127; in each aligned block of 1536 rows (0 to 1535, 1536 to 3071, ...) at most 24 rows name the same one
- far_target_half: int32 [196608], P(('sec', 'az')), may hold values from 0 to 1
- far_source_half: int32 [196608], P(('sec', 'az')), may hold values from 0 to 1
Outputs:
- updated: float32 [256, 16, 1024], P(('sec', 'az'))
The draws below stay inside these ranges and needn't reach their ends.
Inputs may be any that keep to these rules, and one draw needn't show every extreme that they name: `far_target_device`: in the rows of one device's far couplings no device is named more than 24 times, and some device exactly 24 times. `counts`: A multiple of 128; some subdomain has exactly 1024.
All inputs are finite; a program needn't handle non-finite values.
Results may differ from the reference program's by a relative error of at most 0.005.
Values may be sent and summed in bfloat16 or wider, within the bound.
No kernel may reach another device: no remote copies, remote signals or barrier semaphores. Data moves between devices by JAX's collectives and lax.ppermute only.
A program may use at most 64 MiB of HBM per device.

```python
import math
import jax
import jax.numpy as jnp
import numpy as np
from jax import lax

M = 1024
RHS = 16
NEAR_RANK = 128
FAR_RANK = 32
FAR_DEV = 1536
SUBS = 256
CAP = 24
FAR = 196608
N_SEC = 16
N_AZ = 8
DEVICES = 128


def draw_counts(key, part):
    key = jax.random.fold_in(key, 7)
    first_key, second_key = jax.random.split(key)
    tiles = jax.random.randint(first_key, (SUBS,), 1, M // 128 + 1)
    filled = jax.random.randint(second_key, (), 0, SUBS)
    tiles = jnp.where(jnp.arange(SUBS) == filled, M // 128, tiles)
    return (tiles * 128).astype(jnp.int32)


def with_ends(result, own_key, smallest, high):
    index_at = [jax.random.randint(jax.random.fold_in(own_key, axis), (), 0, length) for axis, length in enumerate(result.shape)]
    main_axis = result.shape.index(max(result.shape))
    next_to = index_at[:main_axis] + [(index_at[main_axis] + 1) % result.shape[main_axis]] + index_at[main_axis + 1:]
    return result.at[tuple(index_at)].set(smallest).at[tuple(next_to)].set(high)


def levels(stream_key, shape, pieces, low, high):
    def one(dim, shards_of):
        steps = jax.random.uniform(jax.random.fold_in(jax.random.fold_in(stream_key, 6), dim), (shards_of,), jnp.float32, low / len(pieces), high / len(pieces))
        return jnp.repeat(jnp.exp(steps), shape[dim] // shards_of).reshape((-1,) + (1,) * (len(shape) - dim - 1))

    loudness = one(*pieces[0])
    for cut in pieces[1:]:
        loudness = loudness * one(*cut)
    return loudness


def assign_block(own_key, own, number, rows, amount, top, most, lean):
    order = jax.random.permutation(own_key, amount)
    heavy_load, ordinary = shares(amount, rows * top, most, lean, True), shares(amount, rows * top, most, lean, False)
    places = jnp.arange(amount)

    def named(tallies, rotation):
        used = int((tallies > 0).sum())
        fixed = max(1, used // 4)
        passed = fixed + (places - fixed + rotation * (used - fixed)) % max(1, amount - fixed)
        return jnp.zeros((amount,), jnp.int32).at[order[jnp.where(places < fixed, places, passed)]].set(jnp.asarray(tallies, jnp.int32))

    tallies = jnp.where(number % 4 == 0, named(heavy_load, number // 4), named(ordinary, number - number // 4 - 1))
    mixed = jax.random.permutation(jax.random.fold_in(own, 3), amount)
    donor, sink = mixed[0:amount // 2 * 2:2], mixed[1:amount // 2 * 2:2]
    margin = jnp.minimum(tallies[donor] - 1, most - tallies[sink]) // 2
    margin = jnp.where((donor == order[0]) | (sink == order[0]) | (tallies[sink] == 0), 0, jnp.maximum(margin, 0))
    passed = jax.random.randint(jax.random.fold_in(own, 4), (amount // 2,), 0, 1 << 20) % (margin + 1)
    tallies = tallies.at[donor].add(-passed).at[sink].add(passed)
    items = jnp.searchsorted(jnp.cumsum(tallies), jnp.arange(rows * top), side="right").astype(jnp.int32)
    table = items.reshape(top, rows).T
    table = table[jax.random.permutation(jax.random.fold_in(own, 1), rows)]
    rotation = jax.random.randint(jax.random.fold_in(own, 2), (rows, 1), 0, top)
    return jnp.take_along_axis(table, (jnp.arange(top)[None, :] + rotation) % top, axis=1)


def shares(count, total, most, slope, full):
    loads = [(1 << 20) // math.isqrt(rank ** slope) + 1 for rank in range(1, count + 1)]
    largest = most if full else min(most, max(-(-total // count), total * loads[0] // sum(loads)))
    least = 1 if total - largest >= count - 1 else 0
    given, surplus = [largest] + [least] * (count - 1), total - largest - least * (count - 1)
    while surplus > 0:
        free = [i for i in range(1, count) if given[i] < largest] or [i for i in range(1, count) if given[i] < most]
        whole, left = sum([loads[i] for i in free]), surplus
        for i in free:
            extra = min(most - given[i], max(1, left * loads[i] // whole), surplus)
            given[i] = given[i] + extra
            surplus = surplus - extra
    return np.array(given)


def normal_values(stream_key, extent, scale, reach, pieces=(), dtype=jnp.bfloat16):
    values = scale * jax.random.normal(stream_key, extent, jnp.float32)
    if pieces:
        values = values * levels(stream_key, extent, pieces, -0.22, 0.18)
    return jnp.clip(values, -reach, reach).astype(dtype)


def setup_inputs(seed: int = 0) -> dict:
    key_list = jax.random.split(jax.random.key(seed), 13)
    currents = normal_values(key_list[0], (SUBS, RHS, M), 1.0, 6.0, ((0, 128),), jnp.float32)
    right_side = normal_values(key_list[1], (SUBS, RHS, M), 1.0, 6.0, ((0, 128),), jnp.float32)
    counts = draw_counts(jax.random.fold_in(key_list[12], 71), 0)
    inverse_blocks = normal_values(key_list[3], (SUBS, M, M), M ** -0.5, 0.1875, ((0, 128),))
    near_out = normal_values(key_list[4], (SUBS, 4, NEAR_RANK, M), M ** -0.5, 0.1875, ((0, 128),))
    near_in = normal_values(key_list[5], (SUBS, 4, NEAR_RANK, M), NEAR_RANK ** -0.5, 0.5, ((0, 128),))
    far_source_basis = normal_values(key_list[6], (SUBS, FAR_RANK, M), M ** -0.5, 0.1875, ((0, 128),))
    far_target_basis = normal_values(key_list[7], (SUBS, FAR_RANK, M), FAR_RANK ** -0.5, 1.0, ((0, 128),))
    far_cores = normal_values(key_list[8], (FAR, FAR_RANK * FAR_RANK), (FAR_RANK * FAR_DEV // 2) ** -0.5, 0.0390625, ((0, 128),))
    far_target_device_keys = jax.random.split(jax.random.fold_in(key_list[9], 1), FAR // FAR_DEV)
    far_target_device_turns = jax.random.permutation(jax.random.fold_in(key_list[9], 3), FAR // FAR_DEV)
    far_target_device = jax.vmap(lambda own, number: assign_block(jax.random.fold_in(key_list[9], 2), own, number, FAR_DEV, DEVICES, 1, CAP, 2))(far_target_device_keys, far_target_device_turns).reshape((FAR, 1))
    far_target_half = with_ends(jax.random.randint(key_list[10], (FAR,), 0, 2), jax.random.fold_in(key_list[10], 1), 0, 1).astype(jnp.int32)
    far_source_half = with_ends(jax.random.randint(key_list[11], (FAR,), 0, 2), jax.random.fold_in(key_list[11], 1), 0, 1).astype(jnp.int32)
    return {"currents": currents, "right_side": right_side, "counts": counts, "inverse_blocks": inverse_blocks, "near_out": near_out, "near_in": near_in, "far_source_basis": far_source_basis, "far_target_basis": far_target_basis, "far_cores": far_cores, "far_target_device": far_target_device, "far_target_half": far_target_half, "far_source_half": far_source_half}


def reference(currents, right_side, counts, inverse_blocks, near_out, near_in, far_source_basis, far_target_basis, far_cores, far_target_device, far_target_half, far_source_half):
    row_mask = jnp.arange(M)[None, None, :] < counts[:, None, None]
    masked = jnp.where(row_mask, currents, 0.0).astype(jnp.bfloat16)

    def project(pair):
        return jnp.einsum('rm,dkm->drk', pair[0].astype(jnp.float32), pair[1].astype(jnp.float32), precision=lax.Precision.HIGHEST)

    coeffs = lax.map(project, (masked, near_out)).astype(jnp.bfloat16)
    grid = coeffs.reshape(N_SEC, N_AZ, 2, 4, RHS, NEAR_RANK).transpose(0, 2, 1, 3, 4, 5).reshape(2 * N_SEC, N_AZ, 4, RHS, NEAR_RANK)
    zero_row = jnp.zeros((1, N_AZ, RHS, NEAR_RANK), jnp.bfloat16)
    from_minus = jnp.concatenate([zero_row, grid[:-1, :, 0]], axis=0)
    from_plus = jnp.concatenate([grid[1:, :, 1], zero_row], axis=0)
    from_west = jnp.roll(grid[:, :, 2], 1, axis=1)
    from_east = jnp.roll(grid[:, :, 3], -1, axis=1)
    incoming = jnp.stack([from_minus, from_plus, from_west, from_east], axis=2)
    incoming = incoming.reshape(N_SEC, 2, N_AZ, 4, RHS, NEAR_RANK).transpose(0, 2, 1, 3, 4, 5).reshape(SUBS, 4, RHS, NEAR_RANK)

    def far_project(pair):
        return jnp.dot(pair[0], pair[1].T, preferred_element_type=jnp.float32)

    projected = lax.map(far_project, (masked, far_source_basis)).astype(jnp.bfloat16)
    owner = (jnp.arange(FAR) // FAR_DEV).astype(jnp.int32)
    source_index = (owner * 2 + far_source_half).astype(jnp.int32)
    target_index = (far_target_device[:, 0] * 2 + far_target_half).astype(jnp.int32)
    source_rows = projected[source_index]
    core_mats = far_cores.reshape(FAR, FAR_RANK, FAR_RANK)

    def far_block(pair):
        return jnp.einsum('erj,eij->eri', pair[0].astype(jnp.float32), pair[1].astype(jnp.float32), precision=lax.Precision.HIGHEST).astype(jnp.bfloat16)

    far_terms = lax.map(far_block, (source_rows.reshape(DEVICES, FAR_DEV, RHS, FAR_RANK), core_mats.reshape(DEVICES, FAR_DEV, FAR_RANK, FAR_RANK)))
    far_terms = far_terms.reshape(FAR, RHS, FAR_RANK)
    far_sum = jax.ops.segment_sum(far_terms.astype(jnp.float32), target_index, num_segments=SUBS)
    far_in = far_sum.astype(jnp.bfloat16)
    source_field = jnp.where(row_mask, right_side, 0.0)

    def finish(items):
        inc, factors, far_piece, basis, field, inverse = items
        near_term = jnp.einsum('drk,dkm->rm', inc.astype(jnp.float32), factors.astype(jnp.float32), precision=lax.Precision.HIGHEST)
        far_term = jnp.dot(far_piece, basis, preferred_element_type=jnp.float32)
        residual = (field - near_term - far_term).astype(jnp.bfloat16)
        return jnp.dot(residual, inverse.T, preferred_element_type=jnp.float32)

    updated = lax.map(finish, (incoming, near_in, far_in, far_target_basis, source_field, inverse_blocks))
    return jnp.where(row_mask, updated, 0.0)
```

```python
import jax
import jax.numpy as jnp
from jax import lax
from jax.experimental import pallas as pl
from jax.experimental.pallas import tpu as pltpu
from jax.sharding import PartitionSpec as P

BF = jnp.bfloat16
F32 = jnp.float32
VMEM = pl.BlockSpec(memory_space=pltpu.VMEM)
SMEM = pl.BlockSpec(memory_space=pltpu.SMEM)
ANY = pl.BlockSpec(memory_space=pl.ANY)
MIB = 1024 * 1024
NT = (((1,), (1,)), ((), ()))


def iota(shape, dim):
    return lax.broadcasted_iota(jnp.int32, shape, dim)


def dot(a, b, dims=(((1,), (0,)), ((), ()))):
    return lax.dot_general(a, b, dims, preferred_element_type=F32)


def keep_rows(counts, values, sub):
    return jnp.where(iota(values.shape, 1) < counts[sub], values, 0.0)


def far_out_kernel(counts, currents, basis, device, target_half, source_half, cores_hbm, out, cores, staged, sems):
    chunks, _, width = cores.shape
    rhs_count = currents.shape[1]
    rank = basis.shape[1]
    targets = staged.shape[0] // chunks
    copies = [
        pltpu.make_async_copy(cores_hbm.at[:, pl.ds(k * width, width)], cores.at[k], sems.at[k]) for k in range(chunks)
    ]
    for copy in copies:
        copy.start()
    place = source_half[...] * targets + device[...] * 2 + target_half[...]
    place = place.reshape(1, place.shape[-1])
    onehot = (iota((2 * targets, place.shape[1]), 0) == place).astype(BF)
    lanes = staged.shape[1]
    repeat = (iota((rhs_count, lanes), 1) % rhs_count == iota((rhs_count, lanes), 0)).astype(BF)
    diagonal = iota((width, lanes), 0) // rank == iota((width, lanes), 1) // rhs_count
    spread = []
    for sub in range(2):
        masked = keep_rows(counts, currents[sub], sub).astype(BF)
        projected = dot(basis[sub], masked, NT).astype(BF)
        tiled = jnp.concatenate([dot(projected, repeat)] * (width // rank), axis=0)
        spread.append(jnp.where(diagonal, tiled, 0.0).astype(BF))
    for k in range(chunks):
        copies[k].wait()
        sums = dot(onehot, cores[k]).astype(BF)
        terms = dot(sums[:targets], spread[0]) + dot(sums[targets:], spread[1])
        staged[pl.ds(k, targets, stride=chunks), :] = terms
    out[...] = staged[...].reshape(out.shape).astype(BF)


def near_out_kernel(counts, currents, near_out, up, down, west, east, kept):
    rank = up.shape[1]
    for sub in range(2):
        masked = keep_rows(counts, currents[sub], sub).astype(BF)
        factors = near_out[sub].reshape(4 * rank, near_out.shape[3])
        coeffs = dot(masked, factors, NT).astype(BF)
        west[sub] = coeffs[:, 2 * rank : 3 * rank]
        east[sub] = coeffs[:, 3 * rank :]
        if sub == 0:
            kept[0] = coeffs[:, :rank]
            down[...] = coeffs[:, rank : 2 * rank]
        else:
            up[...] = coeffs[:, :rank]
            kept[1] = coeffs[:, rank : 2 * rank]


def solve_kernel(counts, right_side, above, below, west, east, kept, near_in, basis, inverse, base, weights):
    rank = above.shape[1]
    rhs_count = right_side.shape[1]
    for sub in range(2):
        if sub == 0:
            incoming = [above[...], kept[1], west[0], east[0]]
        else:
            incoming = [kept[0], below[...], west[1], east[1]]
        near_term = dot(jnp.concatenate(incoming, axis=1), near_in[sub].reshape(4 * rank, near_in.shape[3]))
        rest = keep_rows(counts, right_side[sub], sub) - near_term
        high = rest.astype(BF)
        low = (rest - high.astype(F32)).astype(BF)
        solved = dot(jnp.concatenate([high, low, basis[sub]], axis=0), inverse[sub], NT)
        base[sub] = solved[:rhs_count] + solved[rhs_count : 2 * rhs_count]
        weights[sub] = solved[2 * rhs_count :].astype(BF)


def far_in_kernel(counts, received, base, weights, out):
    rhs_count = base.shape[1]
    rank = weights.shape[1]
    sums = jnp.sum(received[...].astype(F32), axis=0)
    chunks = sums.shape[0] // 2
    lanes = sums.shape[1]
    own = iota((rhs_count, lanes), 1) % rhs_count == iota((rhs_count, lanes), 0)
    select = (iota((chunks * lanes, rank), 0) // rhs_count == iota((chunks * lanes, rank), 1)).astype(BF)
    for sub in range(2):
        pieces = [jnp.where(own, sums[sub * chunks + k : sub * chunks + k + 1], 0.0) for k in range(chunks)]
        far_in = dot(jnp.concatenate(pieces, axis=1).astype(BF), select).astype(BF)
        out[sub] = keep_rows(counts, base[sub] - dot(far_in, weights[sub]), sub)


def call(kernel, out_shape, in_specs, flops, moved, scratch=()):
    return pl.pallas_call(
        kernel,
        out_shape=out_shape,
        in_specs=in_specs,
        out_specs=jax.tree.map(lambda _: VMEM, out_shape),
        scratch_shapes=scratch,
        compiler_params=pltpu.CompilerParams(vmem_limit_bytes=40 * MIB),
        cost_estimate=pl.CostEstimate(flops=flops, bytes_accessed=moved, transcendentals=0),
    )


def shape(dims, dtype=BF):
    return jax.ShapeDtypeStruct(dims, dtype)


def local(
    currents,
    right_side,
    counts,
    inverse_blocks,
    near_out,
    near_in,
    far_source_basis,
    far_target_basis,
    far_cores,
    far_target_device,
    far_target_half,
    far_source_half,
):
    _, rhs_count, row_count = currents.shape
    far_rank = far_source_basis.shape[1]
    near_rank = near_out.shape[2]
    far_len = far_cores.shape[0]
    sec_count = lax.axis_size("sec")
    az_count = lax.axis_size("az")
    devices = sec_count * az_count
    width = 256
    chunks = far_cores.shape[1] // width
    lanes = width // far_rank * rhs_count

    packed = call(
        far_out_kernel,
        shape((devices, 2 * chunks, lanes)),
        [SMEM, VMEM, VMEM, VMEM, VMEM, VMEM, ANY],
        2 * 4 * devices * far_len * row_count,
        far_cores.size * 2,
        [
            pltpu.VMEM((chunks, far_len, width), BF),
            pltpu.VMEM((2 * devices * chunks, lanes), F32),
            pltpu.SemaphoreType.DMA((chunks,)),
        ],
    )(
        counts,
        currents,
        far_source_basis,
        far_target_device.reshape(1, far_len),
        far_target_half.reshape(1, far_len),
        far_source_half.reshape(1, far_len),
        far_cores,
    )
    received = lax.all_to_all(packed, ("sec", "az"), split_axis=0, concat_axis=0, tiled=True)

    piece = shape((rhs_count, near_rank))
    pair = shape((2, rhs_count, near_rank))
    up, down, west, east, kept = call(
        near_out_kernel,
        (piece, piece, pair, pair, pair),
        [SMEM, VMEM, VMEM],
        2 * near_out.size * rhs_count,
        near_out.size * 2,
    )(counts, currents, near_out)
    above = lax.ppermute(up, "sec", [(s, s + 1) for s in range(sec_count - 1)])
    below = lax.ppermute(down, "sec", [(s + 1, s) for s in range(sec_count - 1)])
    from_west = lax.ppermute(west, "az", [(a, (a + 1) % az_count) for a in range(az_count)])
    from_east = lax.ppermute(east, "az", [((a + 1) % az_count, a) for a in range(az_count)])

    base, weights = call(
        solve_kernel,
        (shape((2, rhs_count, row_count), F32), shape((2, far_rank, row_count))),
        [SMEM] + [VMEM] * 9,
        2 * 2 * inverse_blocks.size * rhs_count,
        inverse_blocks.size * 2 + near_in.size * 2,
    )(counts, right_side, above, below, from_west, from_east, kept, near_in, far_target_basis, inverse_blocks)

    return call(
        far_in_kernel,
        shape((2, rhs_count, row_count), F32),
        [SMEM] + [VMEM] * 3,
        2 * 2 * rhs_count * far_rank * row_count,
        received.size * 2,
    )(counts, received, base, weights)


def solution(mesh):
    in_specs = (
        P(("sec", "az"), None, None),
        P(("sec", "az"), None, None),
        P(("sec", "az")),
        P(("sec", "az"), None, None),
        P(("sec", "az"), None, None, None),
        P(("sec", "az"), None, None, None),
        P(("sec", "az"), None, None),
        P(("sec", "az"), None, None),
        P(("sec", "az"), None),
        P(("sec", "az"), None),
        P(("sec", "az")),
        P(("sec", "az")),
    )
    out_specs = P(("sec", "az"), None, None)
    return jax.shard_map(local, mesh=mesh, in_specs=in_specs, out_specs=out_specs, check_vma=False)
```

```python
import jax
import jax.numpy as jnp
from jax import lax
from jax.experimental import pallas as pl
from jax.experimental.pallas import tpu as pltpu
from jax.sharding import PartitionSpec as P

BF = jnp.bfloat16
F32 = jnp.float32
VMEM = pl.BlockSpec(memory_space=pltpu.VMEM)
HBM = pl.BlockSpec(memory_space=pltpu.HBM)
MIB = 1024 * 1024
NT = (((1,), (1,)), ((), ()))


def iota(shape, dim):
    return lax.broadcasted_iota(jnp.int32, shape, dim)


def dot(a, b, dims=(((1,), (0,)), ((), ()))):
    return lax.dot_general(a, b, dims, preferred_element_type=F32)


def send_kernel(
    counts_hbm, currents_hbm, basis_hbm, device_hbm, target_hbm, source_hbm, near_out_hbm, cores_hbm,
    packed, sec_a, sec_b, az_a, az_b, kept, keep,
    counts, currents, basis, device, target_half, source_half, near, cores, sums, staged, sems,
):
    steps, rows = cores.shape[:2]
    pairs = [
        (counts_hbm, counts),
        (currents_hbm, currents),
        (device_hbm, device),
        (target_hbm, target_half),
        (source_hbm, source_half),
        (basis_hbm, basis),
        (near_out_hbm.at[0], near.at[0]),
        (near_out_hbm.at[1], near.at[1]),
    ]
    pairs += [(cores_hbm.at[pl.ds(step * rows, rows)], cores.at[step]) for step in range(steps)]
    copies = [pltpu.make_async_copy(source, to, sems.at[i]) for i, (source, to) in enumerate(pairs)]
    for copy in copies:
        copy.start()
    for copy in copies[:6]:
        copy.wait()

    rank = sec_a.shape[1]
    coeffs = []
    masked = []
    for sub in range(2):
        keep[sub] = (iota(keep.shape[1:], 1) < counts[sub]).astype(F32)
        masked.append(jnp.where(iota(currents.shape[1:], 1) < counts[sub], currents[sub], 0.0).astype(BF))
    for sub in range(2):
        copies[6 + sub].wait()
        coeffs.append(dot(masked[sub], near[sub].reshape(4 * rank, near.shape[3]), NT))
    sec_even, az_even = even("sec"), even("az")
    kept[0] = coeffs[0][:, :rank].astype(BF)
    kept[1] = coeffs[1][:, rank : 2 * rank].astype(BF)
    to_next, to_previous = coeffs[1][:, :rank], coeffs[0][:, rank : 2 * rank]
    sec_a[...] = choose(sec_even, to_next, to_previous)
    sec_b[...] = choose(sec_even, to_previous, to_next)
    for sub in range(2):
        to_next, to_previous = coeffs[sub][:, 2 * rank : 3 * rank], coeffs[sub][:, 3 * rank :]
        az_a[sub] = choose(az_even, to_next, to_previous)
        az_b[sub] = choose(az_even, to_previous, to_next)

    chunks = packed.shape[1] // 2
    lanes = packed.shape[2]
    rhs_count = currents.shape[1]
    far_rank = basis.shape[1]
    width = cores.shape[2] // chunks
    repeat = (iota((rhs_count, lanes), 1) % rhs_count == iota((rhs_count, lanes), 0)).astype(BF)
    diagonal = iota((width, lanes), 0) // far_rank == iota((width, lanes), 1) // rhs_count
    spread = []
    for sub in range(2):
        projected = dot(basis[sub], masked[sub], NT).astype(BF)
        tiled = jnp.concatenate([dot(projected, repeat)] * (width // far_rank), axis=0)
        spread.append(jnp.where(diagonal, tiled, 0.0).astype(BF))

    targets = 2 * packed.shape[0]
    halves = source_half[...] * targets + target_half[...]
    place = halves.reshape(device.shape) + device[...] * 2
    total = None
    for step in range(steps):
        onehot = (iota((2 * targets, rows), 0) == place[:, step * rows : (step + 1) * rows]).astype(BF)
        copies[8 + step].wait()
        term = dot(onehot, cores[step])
        total = term if step == 0 else total + term
    sums[...] = total.astype(BF)
    for k in range(chunks):
        part = pl.ds(k * width, width)
        terms = dot(sums[:targets, part], spread[0]) + dot(sums[targets:, part], spread[1])
        staged[pl.ds(k, targets, stride=chunks), :] = terms
    packed[...] = staged[...].reshape(packed.shape).astype(BF)


def even(axis):
    return lax.rem(lax.axis_index(axis), 2) == 0


def choose(first, yes, no):
    return jnp.where(first, yes.astype(F32), no.astype(F32)).astype(BF)


def solve_kernel(
    keep, right_side, kept, basis, near_hbm, inverse_hbm, base, near_weights, far_weights, near_in, inverse, sems
):
    parts, rows = inverse.shape[1:3]
    copies = [
        pltpu.make_async_copy(inverse_hbm.at[sub, pl.ds(part * rows, rows)], inverse.at[sub, part], sems.at[sub, part])
        for sub in range(2)
        for part in range(parts)
    ]
    near_copies = [pltpu.make_async_copy(near_hbm.at[sub], near_in.at[sub], sems.at[sub, parts]) for sub in range(2)]
    for copy in near_copies[:1] + copies[:parts] + near_copies[1:] + copies[parts:]:
        copy.start()
    rhs_count = right_side.shape[1]
    far_rank = basis.shape[1]
    near_rows = near_weights.shape[1]
    for sub in range(2):
        near_copies[sub].wait()
        rest = jnp.where(keep[sub] > 0.0, right_side[sub], 0.0) - dot(kept[1 - sub], near_in[sub, 1 - sub])
        high = rest.astype(BF)
        low = (rest - high.astype(F32)).astype(BF)
        factors = [near_in[sub, sub], near_in[sub, 2], near_in[sub, 3]]
        stacked = jnp.concatenate(factors + [high, low, basis[sub]], axis=0)
        for part in range(parts):
            copies[sub * parts + part].wait()
            solved = dot(stacked, inverse[sub, part], NT)
            columns = pl.ds(part * rows, rows)
            near_weights[sub, :, columns] = solved[:near_rows].astype(BF)
            rest = solved[near_rows:]
            base[sub, :, columns] = rest[:rhs_count] + rest[rhs_count : 2 * rhs_count]
            far_weights[pl.ds(sub * far_rank, far_rank), columns] = rest[2 * rhs_count :].astype(BF)


def finish_kernel(keep, received, sec_a, sec_b, az_a, az_b, base, near_weights, far_weights, out):
    rhs_count = base.shape[1]
    rank = far_weights.shape[0] // 2
    sums = jnp.sum(received[...].astype(F32), axis=0)
    chunks = sums.shape[0] // 2
    lanes = sums.shape[1]
    own = iota((rhs_count, lanes), 1) % rhs_count == iota((rhs_count, lanes), 0)
    spaced = [jnp.where(own, sums[row : row + 1], 0.0).astype(BF) for row in range(2 * chunks)]
    spaced = [jnp.concatenate(spaced[sub * chunks : (sub + 1) * chunks], axis=1) for sub in range(2)]
    size = (chunks * lanes, 2 * rank)
    select = (iota(size, 0) // rhs_count == iota(size, 1) % rank).astype(BF)
    far_in = dot(jnp.concatenate(spaced, axis=0), select)
    block = iota(far_in.shape, 0) // rhs_count == iota(far_in.shape, 1) // rank
    far_term = dot(jnp.where(block, far_in, 0.0).astype(BF), far_weights[...])

    sec_even, az_even = even("sec"), even("az")
    section = lax.axis_index("sec")
    above = jnp.where(section == 0, 0.0, choose(sec_even, sec_b[...], sec_a[...]).astype(F32))
    below = jnp.where(section == lax.axis_size("sec") - 1, 0.0, choose(sec_even, sec_a[...], sec_b[...]).astype(F32))
    along = [above.astype(BF), below.astype(BF)]
    for sub in range(2):
        west, east = choose(az_even, az_b[sub], az_a[sub]), choose(az_even, az_a[sub], az_b[sub])
        near_term = dot(jnp.concatenate([along[sub], west, east], axis=1), near_weights[sub])
        updated = base[sub] - near_term - far_term[sub * rhs_count : (sub + 1) * rhs_count]
        out[sub] = jnp.where(keep[sub] > 0.0, updated, 0.0)


def swap(value, axis, start):
    sec_count, az_count = lax.axis_size("sec"), lax.axis_size("az")
    route = []
    for sec in range(sec_count):
        for az in range(az_count):
            if axis == "az":
                step = 1 if (az - start) % 2 == 0 else -1
                to = sec, (az + step) % az_count
            else:
                step = 1 if (sec - start) % 2 == 0 else -1
                to = (sec + step, az) if 0 <= sec + step < sec_count else (sec, az ^ 1)
            route.append((sec * az_count + az, to[0] * az_count + to[1]))
    return lax.ppermute(value, ("sec", "az"), route)


def in_hbm(array):
    return pltpu.with_memory_space_constraint(array, pltpu.HBM)


def call(kernel, out_shape, in_specs, flops, moved, grant, scratch=()):
    return pl.pallas_call(
        kernel,
        out_shape=out_shape,
        in_specs=in_specs,
        out_specs=jax.tree.map(lambda _: VMEM, out_shape),
        scratch_shapes=scratch,
        compiler_params=pltpu.CompilerParams(vmem_limit_bytes=grant * MIB),
        cost_estimate=pl.CostEstimate(flops=flops, bytes_accessed=moved, transcendentals=0),
    )


def shape(dims, dtype=BF):
    return jax.ShapeDtypeStruct(dims, dtype)


def local(
    currents,
    right_side,
    counts,
    inverse_blocks,
    near_out,
    near_in,
    far_source_basis,
    far_target_basis,
    far_cores,
    far_target_device,
    far_target_half,
    far_source_half,
):
    _, rhs_count, row_count = currents.shape
    far_rank = far_source_basis.shape[1]
    near_rank = near_out.shape[2]
    far_len = far_cores.shape[0]
    sec_count = lax.axis_size("sec")
    az_count = lax.axis_size("az")
    devices = sec_count * az_count
    width = 256
    chunks = far_cores.shape[1] // width
    lanes = width // far_rank * rhs_count

    piece = shape((rhs_count, near_rank))
    pair = shape((2, rhs_count, near_rank))
    steps = 3
    fetched = [counts, currents, far_source_basis, far_target_device.reshape(1, far_len), far_target_half, far_source_half]
    fetched += [near_out, far_cores]
    packed, sec_a, sec_b, az_a, az_b, kept, keep = call(
        send_kernel,
        (shape((devices, 2 * chunks, lanes)), piece, piece, pair, pair, pair, shape((2, 1, row_count), F32)),
        [HBM] * 8,
        2 * 4 * devices * far_len * row_count,
        2 * (far_cores.size + near_out.size),
        24,
        [
            pltpu.SMEM(counts.shape, jnp.int32),
            pltpu.VMEM(currents.shape, F32),
            pltpu.VMEM(far_source_basis.shape, BF),
            pltpu.VMEM((1, far_len), jnp.int32),
            pltpu.VMEM((far_len,), jnp.int32),
            pltpu.VMEM((far_len,), jnp.int32),
            pltpu.VMEM(near_out.shape, BF),
            pltpu.VMEM((steps, far_len // steps, far_cores.shape[1]), BF),
            pltpu.VMEM((4 * devices, far_cores.shape[1]), BF),
            pltpu.VMEM((2 * devices * chunks, lanes), F32),
            pltpu.SemaphoreType.DMA((8 + steps,)),
        ],
    )(*[in_hbm(x) for x in fetched])
    received = lax.all_to_all(packed, ("sec", "az"), split_axis=0, concat_axis=0, tiled=True)
    sec_a, sec_b = swap(sec_a, "sec", 0), swap(sec_b, "sec", 1)
    az_a, az_b = swap(az_a, "az", 0), swap(az_b, "az", 1)

    parts = 2
    base, near_weights, far_weights = call(
        solve_kernel,
        (
            shape((2, rhs_count, row_count), F32),
            shape((2, 3 * near_rank, row_count)),
            shape((2 * far_rank, row_count)),
        ),
        [VMEM] * 4 + [HBM] * 2,
        2 * inverse_blocks.size * (3 * near_rank + 2 * rhs_count + far_rank),
        inverse_blocks.size * 2,
        16,
        [
            pltpu.VMEM(near_in.shape, BF),
            pltpu.VMEM((2, parts, row_count // parts, row_count), BF),
            pltpu.SemaphoreType.DMA((2, parts + 1)),
        ],
    )(keep, right_side, kept, far_target_basis, in_hbm(near_in), in_hbm(inverse_blocks))

    return call(
        finish_kernel,
        shape((2, rhs_count, row_count), F32),
        [VMEM] * 9,
        2 * 2 * rhs_count * (3 * near_rank + far_rank) * row_count,
        received.size * 2,
        4,
    )(keep, received, sec_a, sec_b, az_a, az_b, base, near_weights, far_weights)


def solution(mesh):
    in_specs = (
        P(("sec", "az"), None, None),
        P(("sec", "az"), None, None),
        P(("sec", "az")),
        P(("sec", "az"), None, None),
        P(("sec", "az"), None, None, None),
        P(("sec", "az"), None, None, None),
        P(("sec", "az"), None, None),
        P(("sec", "az"), None, None),
        P(("sec", "az"), None),
        P(("sec", "az"), None),
        P(("sec", "az")),
        P(("sec", "az")),
    )
    out_specs = P(("sec", "az"), None, None)
    return jax.shard_map(local, mesh=mesh, in_specs=in_specs, out_specs=out_specs, check_vma=False)
```

```python
import jax
import jax.numpy as jnp
from jax import lax
from jax.experimental import pallas as pl
from jax.experimental.pallas import tpu as pltpu
from jax.sharding import PartitionSpec as P

BF = jnp.bfloat16
F32 = jnp.float32
VMEM = pl.BlockSpec(memory_space=pltpu.VMEM)
HBM = pl.BlockSpec(memory_space=pltpu.HBM)
MIB = 1024 * 1024
NT = (((1,), (1,)), ((), ()))


def iota(shape, dim):
    return lax.broadcasted_iota(jnp.int32, shape, dim)


def dot(a, b, dims=(((1,), (0,)), ((), ()))):
    return lax.dot_general(a, b, dims, preferred_element_type=F32)


def far_out_kernel(
    counts_hbm, currents_hbm, basis_hbm, device_hbm, target_hbm, source_hbm, cores_hbm,
    packed, masked, keep,
    counts, currents, basis, device, target_half, source_half, cores, terms, staged, sems,
):
    steps, rows = cores.shape[:2]
    pairs = [
        (counts_hbm, counts),
        (currents_hbm, currents),
        (basis_hbm, basis),
        (device_hbm, device),
        (target_hbm, target_half),
        (source_hbm, source_half),
    ]
    pairs += [(cores_hbm.at[pl.ds(step * rows, rows)], cores.at[step]) for step in range(steps)]
    copies = [pltpu.make_async_copy(source, to, sems.at[i]) for i, (source, to) in enumerate(pairs)]
    for copy in copies:
        copy.start()
    for copy in copies[:6]:
        copy.wait()

    chunks = packed.shape[1] // 2
    lanes = packed.shape[2]
    rhs_count = currents.shape[1]
    far_rank = basis.shape[1]
    width = cores.shape[2] // chunks
    targets = 2 * packed.shape[0]

    for sub in range(2):
        keep[sub] = (iota(keep.shape[1:], 1) < counts[sub]).astype(F32)
        masked[sub] = jnp.where(iota(currents.shape[1:], 1) < counts[sub], currents[sub], 0.0).astype(BF)
    both_masked = jnp.concatenate([masked[0], masked[1]], axis=0)
    projected = [dot(basis[sub], both_masked, NT).astype(BF) for sub in range(2)]
    size = (2 * rhs_count, 2 * lanes)
    repeat = iota(size, 1) // lanes * rhs_count + iota(size, 1) % rhs_count == iota(size, 0)
    repeat = repeat.astype(BF)
    size = (width, 2 * lanes)
    diagonal = iota(size, 0) // far_rank == iota(size, 1) % lanes // rhs_count
    tiled = [dot(projected[sub], repeat)[:, sub * lanes : (sub + 1) * lanes] for sub in range(2)]
    tiled = jnp.concatenate([jnp.concatenate(tiled, axis=1)] * (width // far_rank), axis=0)
    spread = jnp.where(diagonal, tiled, 0.0).astype(BF)

    source = source_half[...].reshape(device.shape).astype(F32)
    count = device.shape[1]
    second = [
        jnp.broadcast_to(source[:, start : start + lanes], (lanes, lanes)).T > 0.5 for start in range(0, count, lanes)
    ]
    target = device[...] * 2 + target_half[...].reshape(device.shape)
    onehot = (iota((targets, count), 0) == target).astype(BF)

    sums = None
    for step in range(steps + 1):
        if step < steps:
            copies[6 + step].wait()
            for k in range(chunks):
                both = dot(cores[step, :, k * width : (k + 1) * width], spread)
                for part in range(rows // lanes):
                    piece = both[part * lanes : (part + 1) * lanes]
                    chosen = jnp.where(second[step * (rows // lanes) + part], piece[:, lanes:], piece[:, :lanes])
                    terms[pl.ds(step * rows + part * lanes, lanes), pl.ds(k * lanes, lanes)] = chosen.astype(BF)
        if step > 0:
            part = slice((step - 1) * rows, step * rows)
            term = dot(onehot[:, part], terms[part, :])
            sums = term if sums is None else sums + term
    for k in range(chunks):
        staged[pl.ds(k, targets, stride=chunks), :] = sums[:, k * lanes : (k + 1) * lanes]
    packed[...] = staged[...].reshape(packed.shape).astype(BF)


def even(axis):
    return lax.rem(lax.axis_index(axis), 2) == 0


def choose(first, yes, no):
    return jnp.where(first, yes.astype(F32), no.astype(F32)).astype(BF)


def near_out_kernel(masked, near, sec_a, sec_b, az_a, az_b, kept):
    rank = sec_a.shape[1]
    sec_even, az_even = even("sec"), even("az")
    coeffs = []
    for sub in range(2):
        coeffs.append(dot(masked[sub], near[sub].reshape(4 * rank, near.shape[3]), NT))
    kept[0] = coeffs[0][:, :rank].astype(BF)
    kept[1] = coeffs[1][:, rank : 2 * rank].astype(BF)
    to_next, to_previous = coeffs[1][:, :rank], coeffs[0][:, rank : 2 * rank]
    sec_a[...] = choose(sec_even, to_next, to_previous)
    sec_b[...] = choose(sec_even, to_previous, to_next)
    for sub in range(2):
        to_next, to_previous = coeffs[sub][:, 2 * rank : 3 * rank], coeffs[sub][:, 3 * rank :]
        az_a[sub] = choose(az_even, to_next, to_previous)
        az_b[sub] = choose(az_even, to_previous, to_next)


def solve_kernel(
    keep, right_side, kept, basis, near_in, inverse_hbm, base, near_weights, far_weights, inverse, sems
):
    parts, rows = inverse.shape[1:3]
    copies = [
        pltpu.make_async_copy(inverse_hbm.at[sub, pl.ds(part * rows, rows)], inverse.at[sub, part], sems.at[sub, part])
        for sub in range(2)
        for part in range(parts)
    ]
    for copy in copies:
        copy.start()
    rhs_count = right_side.shape[1]
    far_rank = basis.shape[1]
    near_rows = near_weights.shape[1]
    for sub in range(2):
        rest = jnp.where(keep[sub] > 0.0, right_side[sub], 0.0) - dot(kept[1 - sub], near_in[sub, 1 - sub])
        high = rest.astype(BF)
        low = (rest - high.astype(F32)).astype(BF)
        factors = [near_in[sub, sub], near_in[sub, 2], near_in[sub, 3]]
        stacked = jnp.concatenate(factors + [high, low, basis[sub]], axis=0)
        for part in range(parts):
            copies[sub * parts + part].wait()
            solved = dot(stacked, inverse[sub, part], NT)
            columns = pl.ds(part * rows, rows)
            near_weights[sub, :, columns] = solved[:near_rows].astype(BF)
            rest = solved[near_rows:]
            base[sub, :, columns] = rest[:rhs_count] + rest[rhs_count : 2 * rhs_count]
            rest = jnp.where(keep[sub, :, part * rows : (part + 1) * rows] > 0.0, rest[2 * rhs_count :], 0.0)
            far_weights[pl.ds(sub * far_rank, far_rank), columns] = rest.astype(BF)


def near_in_kernel(keep, sec_a, sec_b, az_a, az_b, base, near_weights, solved):
    sec_even, az_even = even("sec"), even("az")
    section = lax.axis_index("sec")
    above = jnp.where(section == 0, 0.0, choose(sec_even, sec_b[...], sec_a[...]).astype(F32))
    below = jnp.where(section == lax.axis_size("sec") - 1, 0.0, choose(sec_even, sec_a[...], sec_b[...]).astype(F32))
    along = [above.astype(BF), below.astype(BF)]
    for sub in range(2):
        west, east = choose(az_even, az_b[sub], az_a[sub]), choose(az_even, az_a[sub], az_b[sub])
        near_term = dot(jnp.concatenate([along[sub], west, east], axis=1), near_weights[sub])
        solved[sub] = jnp.where(keep[sub] > 0.0, base[sub] - near_term, 0.0)


def far_in_kernel(received, solved, far_weights, out):
    rhs_count = solved.shape[1]
    rank = far_weights.shape[0] // 2
    sums = jnp.sum(received[...].astype(F32), axis=0)
    chunks = sums.shape[0] // 2
    lanes = sums.shape[1]
    own = iota((rhs_count, lanes), 1) % rhs_count == iota((rhs_count, lanes), 0)
    spaced = [jnp.where(own, sums[row : row + 1], 0.0).astype(BF) for row in range(2 * chunks)]
    spaced = [jnp.concatenate(spaced[sub * chunks : (sub + 1) * chunks], axis=1) for sub in range(2)]
    size = (chunks * lanes, 2 * rank)
    select = (iota(size, 0) // rhs_count == iota(size, 1) % rank).astype(BF)
    far_in = dot(jnp.concatenate(spaced, axis=0), select)
    block = iota(far_in.shape, 0) // rhs_count == iota(far_in.shape, 1) // rank
    far_term = dot(jnp.where(block, far_in, 0.0).astype(BF), far_weights[...])
    for sub in range(2):
        out[sub] = solved[sub] - far_term[sub * rhs_count : (sub + 1) * rhs_count]


def swap(value, axis, start):
    sec_count, az_count = lax.axis_size("sec"), lax.axis_size("az")
    route = []
    for sec in range(sec_count):
        for az in range(az_count):
            if axis == "az":
                step = 1 if (az - start) % 2 == 0 else -1
                to = sec, (az + step) % az_count
            else:
                step = 1 if (sec - start) % 2 == 0 else -1
                to = (sec + step, az) if 0 <= sec + step < sec_count else (sec, az ^ 1)
            route.append((sec * az_count + az, to[0] * az_count + to[1]))
    return lax.ppermute(value, ("sec", "az"), route)


def in_hbm(array):
    return pltpu.with_memory_space_constraint(array, pltpu.HBM)


def call(kernel, out_shape, in_specs, flops, moved, grant, scratch=()):
    return pl.pallas_call(
        kernel,
        out_shape=out_shape,
        in_specs=in_specs,
        out_specs=jax.tree.map(lambda _: VMEM, out_shape),
        scratch_shapes=scratch,
        compiler_params=pltpu.CompilerParams(vmem_limit_bytes=grant * MIB),
        cost_estimate=pl.CostEstimate(flops=flops, bytes_accessed=moved, transcendentals=0),
    )


def shape(dims, dtype=BF):
    return jax.ShapeDtypeStruct(dims, dtype)


def local(
    currents,
    right_side,
    counts,
    inverse_blocks,
    near_out,
    near_in,
    far_source_basis,
    far_target_basis,
    far_cores,
    far_target_device,
    far_target_half,
    far_source_half,
):
    _, rhs_count, row_count = currents.shape
    far_rank = far_source_basis.shape[1]
    near_rank = near_out.shape[2]
    far_len = far_cores.shape[0]
    sec_count = lax.axis_size("sec")
    az_count = lax.axis_size("az")
    devices = sec_count * az_count
    width = 256
    chunks = far_cores.shape[1] // width
    lanes = width // far_rank * rhs_count

    piece = shape((rhs_count, near_rank))
    pair = shape((2, rhs_count, near_rank))
    steps = 3
    fetched = [counts, currents, far_source_basis, far_target_device.reshape(1, far_len), far_target_half, far_source_half]
    packed, masked, keep = call(
        far_out_kernel,
        (shape((devices, 2 * chunks, lanes)), shape(currents.shape), shape((2, 1, row_count), F32)),
        [HBM] * 7,
        2 * 2 * devices * far_len * row_count,
        2 * far_cores.size,
        20,
        [
            pltpu.SMEM(counts.shape, jnp.int32),
            pltpu.VMEM(currents.shape, F32),
            pltpu.VMEM(far_source_basis.shape, BF),
            pltpu.VMEM((1, far_len), jnp.int32),
            pltpu.VMEM((far_len,), jnp.int32),
            pltpu.VMEM((far_len,), jnp.int32),
            pltpu.VMEM((steps, far_len // steps, far_cores.shape[1]), BF),
            pltpu.VMEM((far_len, chunks * lanes), BF),
            pltpu.VMEM((2 * devices * chunks, lanes), F32),
            pltpu.SemaphoreType.DMA((6 + steps,)),
        ],
    )(*[in_hbm(x) for x in fetched + [far_cores]])
    received = lax.all_to_all(packed, ("sec", "az"), split_axis=0, concat_axis=0, tiled=True)

    sec_a, sec_b, az_a, az_b, kept = call(
        near_out_kernel,
        (piece, piece, pair, pair, pair),
        [VMEM] * 2,
        2 * near_out.size * rhs_count,
        near_out.size * 2,
        2,
    )(masked, near_out)
    sec_a, sec_b = swap(sec_a, "sec", 0), swap(sec_b, "sec", 1)
    az_a, az_b = swap(az_a, "az", 0), swap(az_b, "az", 1)

    parts = 2
    base, near_weights, far_weights = call(
        solve_kernel,
        (
            shape((2, rhs_count, row_count), F32),
            shape((2, 3 * near_rank, row_count)),
            shape((2 * far_rank, row_count)),
        ),
        [VMEM] * 5 + [HBM],
        2 * inverse_blocks.size * (3 * near_rank + 2 * rhs_count + far_rank),
        inverse_blocks.size * 2,
        16,
        [
            pltpu.VMEM((2, parts, row_count // parts, row_count), BF),
            pltpu.SemaphoreType.DMA((2, parts)),
        ],
    )(keep, right_side, kept, far_target_basis, near_in, in_hbm(inverse_blocks))

    solved = call(
        near_in_kernel,
        shape(right_side.shape, F32),
        [VMEM] * 7,
        2 * 2 * rhs_count * 3 * near_rank * row_count,
        2 * near_in.size,
        4,
    )(keep, sec_a, sec_b, az_a, az_b, base, near_weights)

    return call(
        far_in_kernel,
        shape(right_side.shape, F32),
        [VMEM] * 3,
        2 * 2 * rhs_count * far_rank * row_count,
        received.size * 2,
        4,
    )(received, solved, far_weights)


def solution(mesh):
    in_specs = (
        P(("sec", "az"), None, None),
        P(("sec", "az"), None, None),
        P(("sec", "az")),
        P(("sec", "az"), None, None),
        P(("sec", "az"), None, None, None),
        P(("sec", "az"), None, None, None),
        P(("sec", "az"), None, None),
        P(("sec", "az"), None, None),
        P(("sec", "az"), None),
        P(("sec", "az"), None),
        P(("sec", "az")),
        P(("sec", "az")),
    )
    out_specs = P(("sec", "az"), None, None)
    return jax.shard_map(local, mesh=mesh, in_specs=in_specs, out_specs=out_specs, check_vma=False)
```

```python
import jax
import jax.numpy as jnp
from jax import lax
from jax.experimental import pallas as pl
from jax.experimental.pallas import tpu as pltpu
from jax.sharding import PartitionSpec as P

BF = jnp.bfloat16
F32 = jnp.float32
VMEM = pl.BlockSpec(memory_space=pltpu.VMEM)
HBM = pl.BlockSpec(memory_space=pltpu.HBM)
MIB = 1024 * 1024
NT = (((1,), (1,)), ((), ()))
ALL = ("sec", "y", "core")


def iota(shape, dim):
    return lax.broadcasted_iota(jnp.int32, shape, dim)


def dot(a, b, dims=(((1,), (0,)), ((), ()))):
    return lax.dot_general(a, b, dims, preferred_element_type=F32)


def far_out_kernel(
    counts_hbm, currents_hbm, basis_hbm, device_hbm, target_hbm, source_hbm, cores_hbm,
    packed, masked, keep,
    counts, currents, basis, device, target_half, source_half, cores, terms, staged, sems,
):
    steps, rows = cores.shape[:2]
    pairs = [
        (counts_hbm, counts),
        (currents_hbm, currents),
        (basis_hbm, basis),
        (device_hbm, device),
        (target_hbm, target_half),
        (source_hbm, source_half),
    ]
    pairs += [(cores_hbm.at[pl.ds(step * rows, rows)], cores.at[step]) for step in range(steps)]
    copies = [pltpu.make_async_copy(source, to, sems.at[i]) for i, (source, to) in enumerate(pairs)]
    for copy in copies:
        copy.start()
    for copy in copies[:6]:
        copy.wait()

    chunks = packed.shape[1] // 2
    lanes = packed.shape[2]
    rhs_count = currents.shape[1]
    far_rank = basis.shape[1]
    width = cores.shape[2] // chunks
    targets = 2 * packed.shape[0]

    for sub in range(2):
        keep[sub] = (iota(keep.shape[1:], 1) < counts[sub]).astype(F32)
        masked[sub] = jnp.where(iota(currents.shape[1:], 1) < counts[sub], currents[sub], 0.0).astype(BF)
    both_masked = jnp.concatenate([masked[0], masked[1]], axis=0)
    projected = [dot(basis[sub], both_masked, NT).astype(BF) for sub in range(2)]
    size = (2 * rhs_count, 2 * lanes)
    repeat = iota(size, 1) // lanes * rhs_count + iota(size, 1) % rhs_count == iota(size, 0)
    repeat = repeat.astype(BF)
    size = (width, 2 * lanes)
    diagonal = iota(size, 0) // far_rank == iota(size, 1) % lanes // rhs_count
    tiled = [dot(projected[sub], repeat)[:, sub * lanes : (sub + 1) * lanes] for sub in range(2)]
    tiled = jnp.concatenate([jnp.concatenate(tiled, axis=1)] * (width // far_rank), axis=0)
    spread = jnp.where(diagonal, tiled, 0.0).astype(BF)

    source = source_half[...].reshape(device.shape).astype(F32)
    count = device.shape[1]
    second = [
        jnp.broadcast_to(source[:, start : start + lanes], (lanes, lanes)).T > 0.5 for start in range(0, count, lanes)
    ]
    place = device[...] % 2 * (targets // 4) + device[...] // 2
    target = place * 2 + target_half[...].reshape(device.shape)
    onehot = (iota((targets, count), 0) == target).astype(BF)

    sums = None
    for step in range(steps + 1):
        if step < steps:
            copies[6 + step].wait()
            for k in range(chunks):
                both = dot(cores[step, :, k * width : (k + 1) * width], spread)
                for part in range(rows // lanes):
                    piece = both[part * lanes : (part + 1) * lanes]
                    chosen = jnp.where(second[step * (rows // lanes) + part], piece[:, lanes:], piece[:, :lanes])
                    terms[pl.ds(step * rows + part * lanes, lanes), pl.ds(k * lanes, lanes)] = chosen.astype(BF)
        if step > 0:
            part = slice((step - 1) * rows, step * rows)
            term = dot(onehot[:, part], terms[part, :])
            sums = term if sums is None else sums + term
    for k in range(chunks):
        staged[pl.ds(k, targets, stride=chunks), :] = sums[:, k * lanes : (k + 1) * lanes]
    packed[...] = staged[...].reshape(packed.shape).astype(BF)


def even(axis):
    return lax.axis_index("core") == 0 if axis == "az" else lax.rem(lax.axis_index(axis), 2) == 0


def choose(first, yes, no):
    return jnp.where(first, yes.astype(F32), no.astype(F32)).astype(BF)


def near_out_kernel(masked, near, sec_a, sec_b, az_a, az_b, kept):
    rank = sec_a.shape[1]
    sec_even, az_even = even("sec"), even("az")
    coeffs = []
    for sub in range(2):
        coeffs.append(dot(masked[sub], near[sub].reshape(4 * rank, near.shape[3]), NT))
    kept[0] = coeffs[0][:, :rank].astype(BF)
    kept[1] = coeffs[1][:, rank : 2 * rank].astype(BF)
    to_next, to_previous = coeffs[1][:, :rank], coeffs[0][:, rank : 2 * rank]
    sec_a[...] = choose(sec_even, to_next, to_previous)
    sec_b[...] = choose(sec_even, to_previous, to_next)
    for sub in range(2):
        to_next, to_previous = coeffs[sub][:, 2 * rank : 3 * rank], coeffs[sub][:, 3 * rank :]
        az_a[sub] = choose(az_even, to_next, to_previous)
        az_b[sub] = choose(az_even, to_previous, to_next)


def solve_kernel(
    keep, right_side, kept, basis, near_in, inverse_hbm, base, near_weights, far_weights, inverse, sems
):
    parts, rows = inverse.shape[1:3]
    copies = [
        pltpu.make_async_copy(inverse_hbm.at[sub, pl.ds(part * rows, rows)], inverse.at[sub, part], sems.at[sub, part])
        for sub in range(2)
        for part in range(parts)
    ]
    for copy in copies:
        copy.start()
    rhs_count = right_side.shape[1]
    far_rank = basis.shape[1]
    near_rows = near_weights.shape[1]
    for sub in range(2):
        rest = jnp.where(keep[sub] > 0.0, right_side[sub], 0.0) - dot(kept[1 - sub], near_in[sub, 1 - sub])
        high = rest.astype(BF)
        low = (rest - high.astype(F32)).astype(BF)
        factors = [near_in[sub, sub], near_in[sub, 2], near_in[sub, 3]]
        stacked = jnp.concatenate(factors + [high, low, basis[sub]], axis=0)
        for part in range(parts):
            copies[sub * parts + part].wait()
            solved = dot(stacked, inverse[sub, part], NT)
            columns = pl.ds(part * rows, rows)
            near_weights[sub, :, columns] = solved[:near_rows].astype(BF)
            rest = solved[near_rows:]
            base[sub, :, columns] = rest[:rhs_count] + rest[rhs_count : 2 * rhs_count]
            rest = jnp.where(keep[sub, :, part * rows : (part + 1) * rows] > 0.0, rest[2 * rhs_count :], 0.0)
            far_weights[pl.ds(sub * far_rank, far_rank), columns] = rest.astype(BF)


def near_in_kernel(keep, sec_a, sec_b, az_a, az_b, base, near_weights, solved):
    sec_even, az_even = even("sec"), even("az")
    section = lax.axis_index("sec")
    above = jnp.where(section == 0, 0.0, choose(sec_even, sec_b[...], sec_a[...]).astype(F32))
    below = jnp.where(section == lax.axis_size("sec") - 1, 0.0, choose(sec_even, sec_a[...], sec_b[...]).astype(F32))
    along = [above.astype(BF), below.astype(BF)]
    for sub in range(2):
        west, east = choose(az_even, az_b[sub], az_a[sub]), choose(az_even, az_a[sub], az_b[sub])
        near_term = dot(jnp.concatenate([along[sub], west, east], axis=1), near_weights[sub])
        solved[sub] = jnp.where(keep[sub] > 0.0, base[sub] - near_term, 0.0)


def far_in_kernel(received, solved, far_weights, out):
    rhs_count = solved.shape[1]
    rank = far_weights.shape[0] // 2
    sums = jnp.sum(received[...].astype(F32), axis=0)
    chunks = sums.shape[0] // 2
    lanes = sums.shape[1]
    own = iota((rhs_count, lanes), 1) % rhs_count == iota((rhs_count, lanes), 0)
    spaced = [jnp.where(own, sums[row : row + 1], 0.0).astype(BF) for row in range(2 * chunks)]
    spaced = [jnp.concatenate(spaced[sub * chunks : (sub + 1) * chunks], axis=1) for sub in range(2)]
    size = (chunks * lanes, 2 * rank)
    select = (iota(size, 0) // rhs_count == iota(size, 1) % rank).astype(BF)
    far_in = dot(jnp.concatenate(spaced, axis=0), select)
    block = iota(far_in.shape, 0) // rhs_count == iota(far_in.shape, 1) // rank
    far_term = dot(jnp.where(block, far_in, 0.0).astype(BF), far_weights[...])
    for sub in range(2):
        out[sub] = solved[sub] - far_term[sub * rhs_count : (sub + 1) * rhs_count]


def swap(value, axis, start):
    sec_count, az_count = lax.axis_size("sec"), 2 * lax.axis_size("y")
    route = []
    for sec in range(sec_count):
        for az in range(az_count):
            if axis == "az":
                step = 1 if (az - start) % 2 == 0 else -1
                to = sec, (az + step) % az_count
            else:
                step = 1 if (sec - start) % 2 == 0 else -1
                to = (sec + step, az) if 0 <= sec + step < sec_count else (sec, az ^ 1)
            route.append((sec * az_count + az, to[0] * az_count + to[1]))
    return lax.ppermute(value, ALL, route)


def in_hbm(array):
    return pltpu.with_memory_space_constraint(array, pltpu.HBM)


def call(kernel, out_shape, in_specs, flops, moved, grant, scratch=()):
    return pl.pallas_call(
        kernel,
        out_shape=out_shape,
        in_specs=in_specs,
        out_specs=jax.tree.map(lambda _: VMEM, out_shape),
        scratch_shapes=scratch,
        compiler_params=pltpu.CompilerParams(vmem_limit_bytes=grant * MIB),
        cost_estimate=pl.CostEstimate(flops=flops, bytes_accessed=moved, transcendentals=0),
    )


def shape(dims, dtype=BF):
    return jax.ShapeDtypeStruct(dims, dtype)


def local(
    currents,
    right_side,
    counts,
    inverse_blocks,
    near_out,
    near_in,
    far_source_basis,
    far_target_basis,
    far_cores,
    far_target_device,
    far_target_half,
    far_source_half,
):
    _, rhs_count, row_count = currents.shape
    far_rank = far_source_basis.shape[1]
    near_rank = near_out.shape[2]
    far_len = far_cores.shape[0]
    sec_count = lax.axis_size("sec")
    az_count = 2 * lax.axis_size("y")
    devices = sec_count * az_count
    width = 256
    chunks = far_cores.shape[1] // width
    lanes = width // far_rank * rhs_count

    piece = shape((rhs_count, near_rank))
    pair = shape((2, rhs_count, near_rank))
    steps = 3
    fetched = [counts, currents, far_source_basis, far_target_device.reshape(1, far_len), far_target_half, far_source_half]
    packed, masked, keep = call(
        far_out_kernel,
        (shape((devices, 2 * chunks, lanes)), shape(currents.shape), shape((2, 1, row_count), F32)),
        [HBM] * 7,
        2 * 2 * devices * far_len * row_count,
        2 * far_cores.size,
        20,
        [
            pltpu.SMEM(counts.shape, jnp.int32),
            pltpu.VMEM(currents.shape, F32),
            pltpu.VMEM(far_source_basis.shape, BF),
            pltpu.VMEM((1, far_len), jnp.int32),
            pltpu.VMEM((far_len,), jnp.int32),
            pltpu.VMEM((far_len,), jnp.int32),
            pltpu.VMEM((steps, far_len // steps, far_cores.shape[1]), BF),
            pltpu.VMEM((far_len, chunks * lanes), BF),
            pltpu.VMEM((2 * devices * chunks, lanes), F32),
            pltpu.SemaphoreType.DMA((6 + steps,)),
        ],
    )(*[in_hbm(x) for x in fetched + [far_cores]])
    received = lax.all_to_all(packed, ("core", "sec", "y"), split_axis=0, concat_axis=0, tiled=True)

    sec_a, sec_b, az_a, az_b, kept = call(
        near_out_kernel,
        (piece, piece, pair, pair, pair),
        [VMEM] * 2,
        2 * near_out.size * rhs_count,
        near_out.size * 2,
        2,
    )(masked, near_out)
    sec_a, sec_b = swap(sec_a, "sec", 0), swap(sec_b, "sec", 1)
    az_a, az_b = swap(az_a, "az", 0), swap(az_b, "az", 1)

    parts = 2
    base, near_weights, far_weights = call(
        solve_kernel,
        (
            shape((2, rhs_count, row_count), F32),
            shape((2, 3 * near_rank, row_count)),
            shape((2 * far_rank, row_count)),
        ),
        [VMEM] * 5 + [HBM],
        2 * inverse_blocks.size * (3 * near_rank + 2 * rhs_count + far_rank),
        inverse_blocks.size * 2,
        16,
        [
            pltpu.VMEM((2, parts, row_count // parts, row_count), BF),
            pltpu.SemaphoreType.DMA((2, parts)),
        ],
    )(keep, right_side, kept, far_target_basis, near_in, in_hbm(inverse_blocks))

    solved = call(
        near_in_kernel,
        shape(right_side.shape, F32),
        [VMEM] * 7,
        2 * 2 * rhs_count * 3 * near_rank * row_count,
        2 * near_in.size,
        4,
    )(keep, sec_a, sec_b, az_a, az_b, base, near_weights)

    return call(
        far_in_kernel,
        shape(right_side.shape, F32),
        [VMEM] * 3,
        2 * 2 * rhs_count * far_rank * row_count,
        received.size * 2,
        4,
    )(received, solved, far_weights)


def solution(mesh):
    sec_count, az_count = mesh.devices.shape
    inner = jax.sharding.Mesh(mesh.devices.reshape(sec_count, az_count // 2, 2), ALL)
    in_specs = (P(ALL),) * 12
    return jax.shard_map(local, mesh=inner, in_specs=in_specs, out_specs=P(ALL), check_vma=False)
```

```python
import jax
import jax.numpy as jnp
from jax import lax
from jax.experimental import pallas as pl
from jax.experimental.pallas import tpu as pltpu
from jax.sharding import PartitionSpec as P

BF = jnp.bfloat16
F32 = jnp.float32
VMEM = pl.BlockSpec(memory_space=pltpu.VMEM)
HBM = pl.BlockSpec(memory_space=pltpu.HBM)
MIB = 1024 * 1024
NT = (((1,), (1,)), ((), ()))
ALL = ("sec", "y", "core")


def iota(shape, dim):
    return lax.broadcasted_iota(jnp.int32, shape, dim)


def dot(a, b, dims=(((1,), (0,)), ((), ()))):
    return lax.dot_general(a, b, dims, preferred_element_type=F32)


def send_kernel(
    counts_hbm, currents_hbm, basis_hbm, device_hbm, target_hbm, source_hbm, cores_hbm, near_hbm,
    packed_hbm, sec_a, sec_b, az_a, az_b, kept, keep,
    counts, currents, basis, device, target_half, source_half, cores, near, terms, staged, packed, masked, sems,
):
    steps, rows = cores.shape[:2]
    pairs = [
        (counts_hbm, counts),
        (currents_hbm, currents),
        (basis_hbm, basis),
        (device_hbm, device),
        (target_hbm, target_half),
        (source_hbm, source_half),
    ]
    pairs += [(cores_hbm.at[pl.ds(step * rows, rows)], cores.at[step]) for step in range(steps)]
    pairs += [(near_hbm, near)]
    copies = [pltpu.make_async_copy(source, to, sems.at[i]) for i, (source, to) in enumerate(pairs)]
    for copy in copies:
        copy.start()
    for copy in copies[:6]:
        copy.wait()

    chunks = packed.shape[1] // 2
    lanes = packed.shape[2]
    rhs_count = currents.shape[1]
    far_rank = basis.shape[1]
    width = cores.shape[2] // chunks
    targets = 2 * packed.shape[0]

    for sub in range(2):
        keep[sub] = (iota(keep.shape[1:], 1) < counts[sub]).astype(F32)
        masked[sub] = jnp.where(iota(currents.shape[1:], 1) < counts[sub], currents[sub], 0.0).astype(BF)
    both_masked = jnp.concatenate([masked[0], masked[1]], axis=0)
    projected = [dot(basis[sub], both_masked, NT).astype(BF) for sub in range(2)]
    size = (2 * rhs_count, 2 * lanes)
    repeat = iota(size, 1) // lanes * rhs_count + iota(size, 1) % rhs_count == iota(size, 0)
    repeat = repeat.astype(BF)
    size = (width, 2 * lanes)
    diagonal = iota(size, 0) // far_rank == iota(size, 1) % lanes // rhs_count
    tiled = [dot(projected[sub], repeat)[:, sub * lanes : (sub + 1) * lanes] for sub in range(2)]
    tiled = jnp.concatenate([jnp.concatenate(tiled, axis=1)] * (width // far_rank), axis=0)
    spread = jnp.where(diagonal, tiled, 0.0).astype(BF)

    source = source_half[...].reshape(device.shape).astype(F32)
    count = device.shape[1]
    second = [
        jnp.broadcast_to(source[:, start : start + lanes], (lanes, lanes)).T > 0.5 for start in range(0, count, lanes)
    ]
    place = device[...] % 2 * (targets // 4) + device[...] // 2
    target = place * 2 + target_half[...].reshape(device.shape)
    onehot = (iota((targets, count), 0) == target).astype(BF)

    sums = None
    for step in range(steps + 1):
        if step < steps:
            copies[6 + step].wait()
            for k in range(chunks):
                both = dot(cores[step, :, k * width : (k + 1) * width], spread)
                for part in range(rows // lanes):
                    piece = both[part * lanes : (part + 1) * lanes]
                    chosen = jnp.where(second[step * (rows // lanes) + part], piece[:, lanes:], piece[:, :lanes])
                    terms[pl.ds(step * rows + part * lanes, lanes), pl.ds(k * lanes, lanes)] = chosen.astype(BF)
        if step > 0:
            part = slice((step - 1) * rows, step * rows)
            term = dot(onehot[:, part], terms[part, :])
            sums = term if sums is None else sums + term
    halves = []
    for half in range(2):
        some = targets // 2
        for k in range(chunks):
            piece = sums[half * some : (half + 1) * some, k * lanes : (k + 1) * lanes]
            staged[pl.ds(half * some * chunks + k, some, stride=chunks), :] = piece
        part = pl.ds(half * some // 2, some // 2)
        piece = staged[pl.ds(half * some * chunks, some * chunks), :]
        packed[part] = piece.reshape(some // 2, 2 * chunks, lanes).astype(BF)
        halves.append(pltpu.make_async_copy(packed.at[part], packed_hbm.at[part], sems.at[7 + steps + half]))
        halves[-1].start()

    copies[6 + steps].wait()
    rank = sec_a.shape[1]
    sec_even, az_even = even("sec"), even("az")
    coeffs = []
    for sub in range(2):
        coeffs.append(dot(masked[sub], near[sub].reshape(4 * rank, near.shape[3]), NT))
    kept[0] = coeffs[0][:, :rank].astype(BF)
    kept[1] = coeffs[1][:, rank : 2 * rank].astype(BF)
    to_next, to_previous = coeffs[1][:, :rank], coeffs[0][:, rank : 2 * rank]
    sec_a[...] = choose(sec_even, to_next, to_previous)
    sec_b[...] = choose(sec_even, to_previous, to_next)
    for sub in range(2):
        to_next, to_previous = coeffs[sub][:, 2 * rank : 3 * rank], coeffs[sub][:, 3 * rank :]
        az_a[sub] = choose(az_even, to_next, to_previous)
        az_b[sub] = choose(az_even, to_previous, to_next)
    for copy in halves:
        copy.wait()


def even(axis):
    return lax.axis_index("core") == 0 if axis == "az" else lax.rem(lax.axis_index(axis), 2) == 0


def choose(first, yes, no):
    return jnp.where(first, yes.astype(F32), no.astype(F32)).astype(BF)


def solve_kernel(
    keep, kept, right_hbm, basis_hbm, near_hbm, inverse_hbm,
    base, near_weights, far_weights,
    right_side, basis, near_in, inverse, sems,
):
    parts, rows = inverse.shape[1:3]
    pairs = [(right_hbm, right_side), (basis_hbm, basis)]
    for sub in range(2):
        pairs.append((near_hbm.at[sub], near_in.at[sub]))
        pairs += [(inverse_hbm.at[sub, pl.ds(part * rows, rows)], inverse.at[sub, part]) for part in range(parts)]
    copies = [pltpu.make_async_copy(source, to, sems.at[i]) for i, (source, to) in enumerate(pairs)]
    for copy in copies:
        copy.start()
    for copy in copies[:2]:
        copy.wait()
    rhs_count = right_side.shape[1]
    far_rank = basis.shape[1]
    near_rows = near_weights.shape[1]
    for sub in range(2):
        own = copies[2 + sub * (parts + 1) :]
        own[0].wait()
        rest = jnp.where(keep[sub] > 0.0, right_side[sub], 0.0) - dot(kept[1 - sub], near_in[sub, 1 - sub])
        high = rest.astype(BF)
        low = (rest - high.astype(F32)).astype(BF)
        factors = [near_in[sub, sub], near_in[sub, 2], near_in[sub, 3]]
        stacked = jnp.concatenate(factors + [high, low, basis[sub]], axis=0)
        for part in range(parts):
            own[1 + part].wait()
            solved = dot(stacked, inverse[sub, part], NT)
            columns = pl.ds(part * rows, rows)
            near_weights[sub, :, columns] = solved[:near_rows].astype(BF)
            rest = solved[near_rows:]
            base[sub, :, columns] = rest[:rhs_count] + rest[rhs_count : 2 * rhs_count]
            rest = jnp.where(keep[sub, :, part * rows : (part + 1) * rows] > 0.0, rest[2 * rhs_count :], 0.0)
            far_weights[pl.ds(sub * far_rank, far_rank), columns] = rest.astype(BF)


def near_in_kernel(keep, sec_a, sec_b, az_a, az_b, base, near_weights, solved):
    sec_even, az_even = even("sec"), even("az")
    section = lax.axis_index("sec")
    above = jnp.where(section == 0, 0.0, choose(sec_even, sec_b[...], sec_a[...]).astype(F32))
    below = jnp.where(section == lax.axis_size("sec") - 1, 0.0, choose(sec_even, sec_a[...], sec_b[...]).astype(F32))
    along = [above.astype(BF), below.astype(BF)]
    for sub in range(2):
        west, east = choose(az_even, az_b[sub], az_a[sub]), choose(az_even, az_a[sub], az_b[sub])
        near_term = dot(jnp.concatenate([along[sub], west, east], axis=1), near_weights[sub])
        solved[sub] = jnp.where(keep[sub] > 0.0, base[sub] - near_term, 0.0)


def far_in_kernel(received, solved, far_weights, out):
    rhs_count = solved.shape[1]
    rank = far_weights.shape[0] // 2
    sums = jnp.sum(received[...].astype(F32), axis=0)
    chunks = sums.shape[0] // 2
    lanes = sums.shape[1]
    own = iota((rhs_count, lanes), 1) % rhs_count == iota((rhs_count, lanes), 0)
    spaced = [jnp.where(own, sums[row : row + 1], 0.0).astype(BF) for row in range(2 * chunks)]
    spaced = [jnp.concatenate(spaced[sub * chunks : (sub + 1) * chunks], axis=1) for sub in range(2)]
    size = (chunks * lanes, 2 * rank)
    select = (iota(size, 0) // rhs_count == iota(size, 1) % rank).astype(BF)
    far_in = dot(jnp.concatenate(spaced, axis=0), select)
    block = iota(far_in.shape, 0) // rhs_count == iota(far_in.shape, 1) // rank
    far_term = dot(jnp.where(block, far_in, 0.0).astype(BF), far_weights[...])
    for sub in range(2):
        out[sub] = solved[sub] - far_term[sub * rhs_count : (sub + 1) * rhs_count]


def swap(value, axis, start):
    sec_count, az_count = lax.axis_size("sec"), 2 * lax.axis_size("y")
    route = []
    for sec in range(sec_count):
        for az in range(az_count):
            if axis == "az":
                step = 1 if (az - start) % 2 == 0 else -1
                to = sec, (az + step) % az_count
            else:
                step = 1 if (sec - start) % 2 == 0 else -1
                to = (sec + step, az) if 0 <= sec + step < sec_count else (sec, az ^ 1)
            route.append((sec * az_count + az, to[0] * az_count + to[1]))
    return lax.ppermute(value, ALL, route)


def in_hbm(array):
    return pltpu.with_memory_space_constraint(array, pltpu.HBM)


def call(kernel, out_shape, in_specs, flops, moved, grant, scratch=(), out_specs=None):
    return pl.pallas_call(
        kernel,
        out_shape=out_shape,
        in_specs=in_specs,
        out_specs=out_specs or jax.tree.map(lambda _: VMEM, out_shape),
        scratch_shapes=scratch,
        compiler_params=pltpu.CompilerParams(vmem_limit_bytes=grant * MIB),
        cost_estimate=pl.CostEstimate(flops=flops, bytes_accessed=moved, transcendentals=0),
    )


def shape(dims, dtype=BF):
    return jax.ShapeDtypeStruct(dims, dtype)


def local(
    currents,
    right_side,
    counts,
    inverse_blocks,
    near_out,
    near_in,
    far_source_basis,
    far_target_basis,
    far_cores,
    far_target_device,
    far_target_half,
    far_source_half,
):
    _, rhs_count, row_count = currents.shape
    far_rank = far_source_basis.shape[1]
    near_rank = near_out.shape[2]
    far_len = far_cores.shape[0]
    sec_count = lax.axis_size("sec")
    az_count = 2 * lax.axis_size("y")
    devices = sec_count * az_count
    width = 256
    chunks = far_cores.shape[1] // width
    lanes = width // far_rank * rhs_count

    piece = shape((rhs_count, near_rank))
    pair = shape((2, rhs_count, near_rank))
    steps = 3
    fetched = [counts, currents, far_source_basis, far_target_device.reshape(1, far_len), far_target_half, far_source_half]
    packed, sec_a, sec_b, az_a, az_b, kept, keep = call(
        send_kernel,
        (
            shape((devices, 2 * chunks, lanes)),
            piece,
            piece,
            pair,
            pair,
            pair,
            shape((2, 1, row_count), F32),
        ),
        [HBM] * 8,
        2 * 2 * devices * far_len * row_count,
        2 * far_cores.size,
        20,
        [
            pltpu.SMEM(counts.shape, jnp.int32),
            pltpu.VMEM(currents.shape, F32),
            pltpu.VMEM(far_source_basis.shape, BF),
            pltpu.VMEM((1, far_len), jnp.int32),
            pltpu.VMEM((far_len,), jnp.int32),
            pltpu.VMEM((far_len,), jnp.int32),
            pltpu.VMEM((steps, far_len // steps, far_cores.shape[1]), BF),
            pltpu.VMEM(near_out.shape, BF),
            pltpu.VMEM((far_len, chunks * lanes), BF),
            pltpu.VMEM((2 * devices * chunks, lanes), F32),
            pltpu.VMEM((devices, 2 * chunks, lanes), BF),
            pltpu.VMEM(currents.shape, BF),
            pltpu.SemaphoreType.DMA((9 + steps,)),
        ],
        (HBM,) + (VMEM,) * 6,
    )(*[in_hbm(x) for x in fetched + [far_cores, near_out]])
    received = lax.all_to_all(packed, ("core", "sec", "y"), split_axis=0, concat_axis=0, tiled=True)
    sec_a, sec_b = swap(sec_a, "sec", 0), swap(sec_b, "sec", 1)
    az_a, az_b = swap(az_a, "az", 0), swap(az_b, "az", 1)

    parts = 2
    base, near_weights, far_weights = call(
        solve_kernel,
        (
            shape((2, rhs_count, row_count), F32),
            shape((2, 3 * near_rank, row_count)),
            shape((2 * far_rank, row_count)),
        ),
        [VMEM] * 2 + [HBM] * 4,
        2 * inverse_blocks.size * (3 * near_rank + 2 * rhs_count + far_rank),
        inverse_blocks.size * 2,
        16,
        [
            pltpu.VMEM(right_side.shape, F32),
            pltpu.VMEM(far_target_basis.shape, BF),
            pltpu.VMEM(near_in.shape, BF),
            pltpu.VMEM((2, parts, row_count // parts, row_count), BF),
            pltpu.SemaphoreType.DMA((4 + 2 * parts,)),
        ],
    )(keep, kept, *[in_hbm(x) for x in [right_side, far_target_basis, near_in, inverse_blocks]])

    solved = call(
        near_in_kernel,
        shape(right_side.shape, F32),
        [VMEM] * 7,
        2 * 2 * rhs_count * 3 * near_rank * row_count,
        2 * near_in.size,
        4,
    )(keep, sec_a, sec_b, az_a, az_b, base, near_weights)

    return call(
        far_in_kernel,
        shape(right_side.shape, F32),
        [VMEM] * 3,
        2 * 2 * rhs_count * far_rank * row_count,
        received.size * 2,
        4,
    )(received, solved, far_weights)


def solution(mesh):
    sec_count, az_count = mesh.devices.shape
    inner = jax.sharding.Mesh(mesh.devices.reshape(sec_count, az_count // 2, 2), ALL)
    in_specs = (P(ALL),) * 12
    return jax.shard_map(local, mesh=inner, in_specs=in_specs, out_specs=P(ALL), check_vma=False)
```

```python
import jax
import jax.numpy as jnp
from jax import lax
from jax.experimental import pallas as pl
from jax.experimental.pallas import tpu as pltpu
from jax.sharding import PartitionSpec as P

BF = jnp.bfloat16
F32 = jnp.float32
VMEM = pl.BlockSpec(memory_space=pltpu.VMEM)
HBM = pl.BlockSpec(memory_space=pltpu.HBM)
MIB = 1024 * 1024
NT = (((1,), (1,)), ((), ()))
ALL = ("sec", "y", "core")


def iota(shape, dim):
    return lax.broadcasted_iota(jnp.int32, shape, dim)


def dot(a, b, dims=(((1,), (0,)), ((), ()))):
    return lax.dot_general(a, b, dims, preferred_element_type=F32)


def send_kernel(
    counts_hbm, currents_hbm, basis_hbm, device_hbm, target_hbm, source_hbm, cores_hbm, near_hbm,
    packed_hbm, sec_a, sec_b, az_a, az_b, kept, keep,
    counts, currents, basis, device, target_half, source_half, cores, near, terms, staged, packed, masked, sems,
):
    steps, rows = cores.shape[:2]
    pairs = [
        (counts_hbm, counts),
        (currents_hbm, currents),
        (basis_hbm, basis),
        (device_hbm, device),
        (target_hbm, target_half),
        (source_hbm, source_half),
    ]
    pairs += [(cores_hbm.at[pl.ds(step * rows, rows)], cores.at[step]) for step in range(steps)]
    pairs += [(near_hbm, near)]
    copies = [pltpu.make_async_copy(source, to, sems.at[i]) for i, (source, to) in enumerate(pairs)]
    for copy in copies:
        copy.start()
    for copy in copies[:6]:
        copy.wait()

    chunks = packed.shape[1] // 2
    lanes = packed.shape[2]
    rhs_count = currents.shape[1]
    far_rank = basis.shape[1]
    width = cores.shape[2] // chunks
    targets = 2 * packed.shape[0]

    for sub in range(2):
        keep[sub] = (iota(keep.shape[1:], 1) < counts[sub]).astype(F32)
        masked[sub] = jnp.where(iota(currents.shape[1:], 1) < counts[sub], currents[sub], 0.0).astype(BF)
    both_masked = jnp.concatenate([masked[0], masked[1]], axis=0)
    projected = [dot(basis[sub], both_masked, NT).astype(BF) for sub in range(2)]
    size = (2 * rhs_count, 2 * lanes)
    repeat = iota(size, 1) // lanes * rhs_count + iota(size, 1) % rhs_count == iota(size, 0)
    repeat = repeat.astype(BF)
    size = (width, 2 * lanes)
    diagonal = iota(size, 0) // far_rank == iota(size, 1) % lanes // rhs_count
    tiled = [dot(projected[sub], repeat)[:, sub * lanes : (sub + 1) * lanes] for sub in range(2)]
    tiled = jnp.concatenate([jnp.concatenate(tiled, axis=1)] * (width // far_rank), axis=0)
    spread = jnp.where(diagonal, tiled, 0.0).astype(BF)

    source = source_half[...].reshape(device.shape).astype(F32)
    count = device.shape[1]
    second = [
        jnp.broadcast_to(source[:, start : start + lanes], (lanes, lanes)).T > 0.5 for start in range(0, count, lanes)
    ]
    place = device[...] % 2 * (targets // 4) + device[...] // 2
    target = place * 2 + target_half[...].reshape(device.shape)
    onehot = (iota((targets, count), 0) == target).astype(BF)

    sums = None
    for step in range(steps + 1):
        if step < steps:
            copies[6 + step].wait()
            for k in range(chunks):
                both = dot(cores[step, :, k * width : (k + 1) * width], spread)
                for part in range(rows // lanes):
                    piece = both[part * lanes : (part + 1) * lanes]
                    chosen = jnp.where(second[step * (rows // lanes) + part], piece[:, lanes:], piece[:, :lanes])
                    terms[pl.ds(step * rows + part * lanes, lanes), pl.ds(k * lanes, lanes)] = chosen.astype(BF)
        if step > 0:
            part = slice((step - 1) * rows, step * rows)
            term = dot(onehot[:, part], terms[part, :])
            sums = term if sums is None else sums + term
    for k in range(chunks):
        staged[pl.ds(k, targets, stride=chunks), :] = sums[:, k * lanes : (k + 1) * lanes]
    packed[...] = staged[: targets * chunks, :].reshape(packed.shape).astype(BF)
    sent = pltpu.make_async_copy(packed, packed_hbm, sems.at[7 + steps])
    sent.start()

    copies[6 + steps].wait()
    rank = sec_a.shape[1]
    sec_even, az_even = even("sec"), even("az")
    coeffs = []
    for sub in range(2):
        coeffs.append(dot(masked[sub], near[sub].reshape(4 * rank, near.shape[3]), NT))
    kept[0] = coeffs[0][:, :rank].astype(BF)
    kept[1] = coeffs[1][:, rank : 2 * rank].astype(BF)
    to_next, to_previous = coeffs[1][:, :rank], coeffs[0][:, rank : 2 * rank]
    sec_a[...] = choose(sec_even, to_next, to_previous)
    sec_b[...] = choose(sec_even, to_previous, to_next)
    for sub in range(2):
        to_next, to_previous = coeffs[sub][:, 2 * rank : 3 * rank], coeffs[sub][:, 3 * rank :]
        az_a[sub] = choose(az_even, to_next, to_previous)
        az_b[sub] = choose(az_even, to_previous, to_next)
    sent.wait()


def even(axis):
    return lax.axis_index("core") == 0 if axis == "az" else lax.rem(lax.axis_index(axis), 2) == 0


def choose(first, yes, no):
    return jnp.where(first, yes.astype(F32), no.astype(F32)).astype(BF)


def solve_kernel(
    keep, kept, right_hbm, basis_hbm, near_hbm, inverse_hbm,
    base, near_weights, far_weights,
    right_side, basis, near_in, inverse, sems,
):
    parts, rows = inverse.shape[1:3]
    pairs = [(right_hbm, right_side), (basis_hbm, basis)]
    for sub in range(2):
        pairs.append((near_hbm.at[sub], near_in.at[sub]))
        pairs += [(inverse_hbm.at[sub, pl.ds(part * rows, rows)], inverse.at[sub, part]) for part in range(parts)]
    copies = [pltpu.make_async_copy(source, to, sems.at[i]) for i, (source, to) in enumerate(pairs)]
    for copy in copies:
        copy.start()
    for copy in copies[:2]:
        copy.wait()
    rhs_count = right_side.shape[1]
    far_rank = basis.shape[1]
    near_rows = near_weights.shape[1]
    for sub in range(2):
        own = copies[2 + sub * (parts + 1) :]
        own[0].wait()
        rest = jnp.where(keep[sub] > 0.0, right_side[sub], 0.0) - dot(kept[1 - sub], near_in[sub, 1 - sub])
        high = rest.astype(BF)
        low = (rest - high.astype(F32)).astype(BF)
        factors = [near_in[sub, sub], near_in[sub, 2], near_in[sub, 3]]
        stacked = jnp.concatenate(factors + [high, low, basis[sub]], axis=0)
        for part in range(parts):
            own[1 + part].wait()
            solved = dot(stacked, inverse[sub, part], NT)
            columns = pl.ds(part * rows, rows)
            near_weights[sub, :, columns] = solved[:near_rows].astype(BF)
            rest = solved[near_rows:]
            base[sub, :, columns] = rest[:rhs_count] + rest[rhs_count : 2 * rhs_count]
            rest = jnp.where(keep[sub, :, part * rows : (part + 1) * rows] > 0.0, rest[2 * rhs_count :], 0.0)
            far_weights[pl.ds(sub * far_rank, far_rank), columns] = rest.astype(BF)


def near_in_kernel(keep, sec_a, sec_b, az_a, az_b, base, near_weights, solved):
    sec_even, az_even = even("sec"), even("az")
    section = lax.axis_index("sec")
    above = jnp.where(section == 0, 0.0, choose(sec_even, sec_b[...], sec_a[...]).astype(F32))
    below = jnp.where(section == lax.axis_size("sec") - 1, 0.0, choose(sec_even, sec_a[...], sec_b[...]).astype(F32))
    along = [above.astype(BF), below.astype(BF)]
    for sub in range(2):
        west, east = choose(az_even, az_b[sub], az_a[sub]), choose(az_even, az_a[sub], az_b[sub])
        near_term = dot(jnp.concatenate([along[sub], west, east], axis=1), near_weights[sub])
        solved[sub] = jnp.where(keep[sub] > 0.0, base[sub] - near_term, 0.0)


def far_in_kernel(received, solved, far_weights, out):
    rhs_count = solved.shape[1]
    rank = far_weights.shape[0] // 2
    sums = jnp.sum(received[...].astype(F32), axis=0)
    chunks = sums.shape[0] // 2
    lanes = sums.shape[1]
    own = iota((rhs_count, lanes), 1) % rhs_count == iota((rhs_count, lanes), 0)
    spaced = [jnp.where(own, sums[row : row + 1], 0.0).astype(BF) for row in range(2 * chunks)]
    spaced = [jnp.concatenate(spaced[sub * chunks : (sub + 1) * chunks], axis=1) for sub in range(2)]
    size = (chunks * lanes, 2 * rank)
    select = (iota(size, 0) // rhs_count == iota(size, 1) % rank).astype(BF)
    far_in = dot(jnp.concatenate(spaced, axis=0), select)
    block = iota(far_in.shape, 0) // rhs_count == iota(far_in.shape, 1) // rank
    far_term = dot(jnp.where(block, far_in, 0.0).astype(BF), far_weights[...])
    for sub in range(2):
        out[sub] = solved[sub] - far_term[sub * rhs_count : (sub + 1) * rhs_count]


def swap(value, axis, start):
    sec_count, az_count = lax.axis_size("sec"), 2 * lax.axis_size("y")
    route = []
    for sec in range(sec_count):
        for az in range(az_count):
            if axis == "az":
                step = 1 if (az - start) % 2 == 0 else -1
                to = sec, (az + step) % az_count
            else:
                step = 1 if (sec - start) % 2 == 0 else -1
                to = (sec + step, az) if 0 <= sec + step < sec_count else (sec, az ^ 1)
            route.append((sec * az_count + az, to[0] * az_count + to[1]))
    return lax.ppermute(value, ALL, route)


def in_hbm(array):
    return pltpu.with_memory_space_constraint(array, pltpu.HBM)


def call(kernel, out_shape, in_specs, flops, moved, grant, scratch=(), out_specs=None):
    return pl.pallas_call(
        kernel,
        out_shape=out_shape,
        in_specs=in_specs,
        out_specs=out_specs or jax.tree.map(lambda _: VMEM, out_shape),
        scratch_shapes=scratch,
        compiler_params=pltpu.CompilerParams(vmem_limit_bytes=grant * MIB),
        cost_estimate=pl.CostEstimate(flops=flops, bytes_accessed=moved, transcendentals=0),
    )


def shape(dims, dtype=BF):
    return jax.ShapeDtypeStruct(dims, dtype)


def local(
    currents,
    right_side,
    counts,
    inverse_blocks,
    near_out,
    near_in,
    far_source_basis,
    far_target_basis,
    far_cores,
    far_target_device,
    far_target_half,
    far_source_half,
):
    _, rhs_count, row_count = currents.shape
    far_rank = far_source_basis.shape[1]
    near_rank = near_out.shape[2]
    far_len = far_cores.shape[0]
    sec_count = lax.axis_size("sec")
    az_count = 2 * lax.axis_size("y")
    devices = sec_count * az_count
    width = 256
    chunks = far_cores.shape[1] // width
    lanes = width // far_rank * rhs_count

    piece = shape((rhs_count, near_rank))
    pair = shape((2, rhs_count, near_rank))
    steps = 3
    fetched = [counts, currents, far_source_basis, far_target_device.reshape(1, far_len), far_target_half, far_source_half]
    packed, sec_a, sec_b, az_a, az_b, kept, keep = call(
        send_kernel,
        (
            shape((devices, 2 * chunks, lanes)),
            piece,
            piece,
            pair,
            pair,
            pair,
            shape((2, 1, row_count), F32),
        ),
        [HBM] * 8,
        2 * 2 * devices * far_len * row_count,
        2 * far_cores.size,
        20,
        [
            pltpu.SMEM(counts.shape, jnp.int32),
            pltpu.VMEM(currents.shape, F32),
            pltpu.VMEM(far_source_basis.shape, BF),
            pltpu.VMEM((1, far_len), jnp.int32),
            pltpu.VMEM((far_len,), jnp.int32),
            pltpu.VMEM((far_len,), jnp.int32),
            pltpu.VMEM((steps, far_len // steps, far_cores.shape[1]), BF),
            pltpu.VMEM(near_out.shape, BF),
            pltpu.VMEM((far_len, chunks * lanes), BF),
            pltpu.VMEM((2 * devices * chunks + 8, lanes), F32),
            pltpu.VMEM((devices, 2 * chunks, lanes), BF),
            pltpu.VMEM(currents.shape, BF),
            pltpu.SemaphoreType.DMA((8 + steps,)),
        ],
        (HBM,) + (VMEM,) * 6,
    )(*[in_hbm(x) for x in fetched + [far_cores, near_out]])
    received = lax.all_to_all(packed, ("core", "sec", "y"), split_axis=0, concat_axis=0, tiled=True)
    sec_a, sec_b = swap(sec_a, "sec", 0), swap(sec_b, "sec", 1)
    az_a, az_b = swap(az_a, "az", 0), swap(az_b, "az", 1)

    parts = 1
    base, near_weights, far_weights = call(
        solve_kernel,
        (
            shape((2, rhs_count, row_count), F32),
            shape((2, 3 * near_rank, row_count)),
            shape((2 * far_rank, row_count)),
        ),
        [VMEM] * 2 + [HBM] * 4,
        2 * inverse_blocks.size * (3 * near_rank + 2 * rhs_count + far_rank),
        inverse_blocks.size * 2,
        16,
        [
            pltpu.VMEM(right_side.shape, F32),
            pltpu.VMEM(far_target_basis.shape, BF),
            pltpu.VMEM(near_in.shape, BF),
            pltpu.VMEM((2, parts, row_count // parts, row_count), BF),
            pltpu.SemaphoreType.DMA((4 + 2 * parts,)),
        ],
    )(keep, kept, *[in_hbm(x) for x in [right_side, far_target_basis, near_in, inverse_blocks]])

    solved = call(
        near_in_kernel,
        shape(right_side.shape, F32),
        [VMEM] * 7,
        2 * 2 * rhs_count * 3 * near_rank * row_count,
        2 * near_in.size,
        4,
    )(keep, sec_a, sec_b, az_a, az_b, base, near_weights)

    return call(
        far_in_kernel,
        shape(right_side.shape, F32),
        [VMEM] * 3,
        2 * 2 * rhs_count * far_rank * row_count,
        received.size * 2,
        4,
    )(received, solved, far_weights)


def solution(mesh):
    sec_count, az_count = mesh.devices.shape
    inner = jax.sharding.Mesh(mesh.devices.reshape(sec_count, az_count // 2, 2), ALL)
    in_specs = (P(ALL),) * 12
    return jax.shard_map(local, mesh=inner, in_specs=in_specs, out_specs=P(ALL), check_vma=False)
```

```python
import jax
import jax.numpy as jnp
from jax import lax
from jax.experimental import pallas as pl
from jax.experimental.pallas import tpu as pltpu
from jax.sharding import PartitionSpec as P

BF = jnp.bfloat16
F32 = jnp.float32
VMEM = pl.BlockSpec(memory_space=pltpu.VMEM)
HBM = pl.BlockSpec(memory_space=pltpu.HBM)
MIB = 1024 * 1024
NT = (((1,), (1,)), ((), ()))
ALL = ("sec", "y", "core")


def iota(shape, dim):
    return lax.broadcasted_iota(jnp.int32, shape, dim)


def dot(a, b, dims=(((1,), (0,)), ((), ()))):
    return lax.dot_general(a, b, dims, preferred_element_type=F32)


def send_kernel(
    counts_hbm, currents_hbm, basis_hbm, device_hbm, target_hbm, source_hbm, cores_hbm, near_hbm,
    packed_hbm, sec_a, sec_b, az_a, az_b, kept, keep,
    counts, currents, basis, device, target_half, source_half, cores, near, terms, staged, packed, masked, sems,
):
    steps, rows = cores.shape[:2]
    pairs = [
        (counts_hbm, counts),
        (currents_hbm, currents),
        (basis_hbm, basis),
        (device_hbm, device),
        (target_hbm, target_half),
        (source_hbm, source_half),
    ]
    pairs += [(cores_hbm.at[pl.ds(step * rows, rows)], cores.at[step]) for step in range(steps)]
    pairs += [(near_hbm, near)]
    copies = [pltpu.make_async_copy(source, to, sems.at[i]) for i, (source, to) in enumerate(pairs)]
    for copy in copies:
        copy.start()
    for copy in copies[:6]:
        copy.wait()

    chunks = packed.shape[1] // 2
    lanes = packed.shape[2]
    rhs_count = currents.shape[1]
    far_rank = basis.shape[1]
    width = cores.shape[2] // chunks
    targets = 2 * packed.shape[0]

    for sub in range(2):
        keep[sub] = (iota(keep.shape[1:], 1) < counts[sub]).astype(F32)
        masked[sub] = jnp.where(iota(currents.shape[1:], 1) < counts[sub], currents[sub], 0.0).astype(BF)
    copied = lanes // rhs_count
    size = (width, lanes)
    diagonal = iota(size, 0) // far_rank == iota(size, 1) // rhs_count
    spread = []
    for sub in range(2):
        projected = dot(basis[sub], jnp.concatenate([masked[sub]] * copied, axis=0), NT)
        tiled = jnp.concatenate([projected] * (width // far_rank), axis=0)
        spread.append(jnp.where(diagonal, tiled, 0.0).astype(BF))
    spread = jnp.concatenate(spread, axis=1)

    source = source_half[...].reshape(device.shape).astype(F32)
    count = device.shape[1]
    second = [
        jnp.broadcast_to(source[:, start : start + lanes], (lanes, lanes)).T > 0.5 for start in range(0, count, lanes)
    ]
    place = device[...] % 2 * (targets // 4) + device[...] // 2
    target = place * 2 + target_half[...].reshape(device.shape)
    onehot = (iota((targets, count), 0) == target).astype(BF)

    sums = None
    for step in range(steps + 1):
        if step < steps:
            copies[6 + step].wait()
            for k in range(chunks):
                both = dot(cores[step, :, k * width : (k + 1) * width], spread)
                for part in range(rows // lanes):
                    piece = both[part * lanes : (part + 1) * lanes]
                    chosen = jnp.where(second[step * (rows // lanes) + part], piece[:, lanes:], piece[:, :lanes])
                    terms[pl.ds(step * rows + part * lanes, lanes), pl.ds(k * lanes, lanes)] = chosen.astype(BF)
        if step > 0:
            part = slice((step - 1) * rows, step * rows)
            term = dot(onehot[:, part], terms[part, :])
            sums = term if sums is None else sums + term
    for k in range(chunks):
        staged[pl.ds(k, targets, stride=chunks), :] = sums[:, k * lanes : (k + 1) * lanes]
    packed[...] = staged[: targets * chunks, :].reshape(packed.shape).astype(BF)
    sent = pltpu.make_async_copy(packed, packed_hbm, sems.at[7 + steps])
    sent.start()

    copies[6 + steps].wait()
    rank = sec_a.shape[1]
    sec_even, az_even = even("sec"), even("az")
    coeffs = []
    for sub in range(2):
        coeffs.append(dot(masked[sub], near[sub].reshape(4 * rank, near.shape[3]), NT))
    kept[0] = coeffs[0][:, :rank].astype(BF)
    kept[1] = coeffs[1][:, rank : 2 * rank].astype(BF)
    to_next, to_previous = coeffs[1][:, :rank], coeffs[0][:, rank : 2 * rank]
    sec_a[...] = choose(sec_even, to_next, to_previous)
    sec_b[...] = choose(sec_even, to_previous, to_next)
    for sub in range(2):
        to_next, to_previous = coeffs[sub][:, 2 * rank : 3 * rank], coeffs[sub][:, 3 * rank :]
        az_a[sub] = choose(az_even, to_next, to_previous)
        az_b[sub] = choose(az_even, to_previous, to_next)
    sent.wait()


def even(axis):
    return lax.axis_index("core") == 0 if axis == "az" else lax.rem(lax.axis_index(axis), 2) == 0


def choose(first, yes, no):
    return jnp.where(first, yes.astype(F32), no.astype(F32)).astype(BF)


def solve_kernel(
    keep, kept, right_hbm, basis_hbm, near_hbm, inverse_hbm,
    base, near_weights, far_weights,
    right_side, basis, near_in, inverse, sems,
):
    parts, rows = inverse.shape[1:3]
    pairs = [(right_hbm, right_side), (basis_hbm, basis)]
    for sub in range(2):
        pairs.append((near_hbm.at[sub], near_in.at[sub]))
        pairs += [(inverse_hbm.at[sub, pl.ds(part * rows, rows)], inverse.at[sub, part]) for part in range(parts)]
    copies = [pltpu.make_async_copy(source, to, sems.at[i]) for i, (source, to) in enumerate(pairs)]
    for copy in copies:
        copy.start()
    for copy in copies[:2]:
        copy.wait()
    rhs_count = right_side.shape[1]
    far_rank = basis.shape[1]
    near_rows = near_weights.shape[1]
    for sub in range(2):
        own = copies[2 + sub * (parts + 1) :]
        own[0].wait()
        rest = jnp.where(keep[sub] > 0.0, right_side[sub], 0.0) - dot(kept[1 - sub], near_in[sub, 1 - sub])
        high = rest.astype(BF)
        low = (rest - high.astype(F32)).astype(BF)
        factors = [near_in[sub, sub], near_in[sub, 2], near_in[sub, 3]]
        stacked = jnp.concatenate(factors + [high, low, basis[sub]], axis=0)
        for part in range(parts):
            own[1 + part].wait()
            solved = dot(stacked, inverse[sub, part], NT)
            columns = pl.ds(part * rows, rows)
            near_weights[sub, :, columns] = solved[:near_rows].astype(BF)
            rest = solved[near_rows:]
            base[sub, :, columns] = rest[:rhs_count] + rest[rhs_count : 2 * rhs_count]
            rest = jnp.where(keep[sub, :, part * rows : (part + 1) * rows] > 0.0, rest[2 * rhs_count :], 0.0)
            far_weights[pl.ds(sub * far_rank, far_rank), columns] = rest.astype(BF)


def near_in_kernel(keep, sec_a, sec_b, az_a, az_b, base, near_weights, solved):
    sec_even, az_even = even("sec"), even("az")
    section = lax.axis_index("sec")
    above = jnp.where(section == 0, 0.0, choose(sec_even, sec_b[...], sec_a[...]).astype(F32))
    below = jnp.where(section == lax.axis_size("sec") - 1, 0.0, choose(sec_even, sec_a[...], sec_b[...]).astype(F32))
    along = [above.astype(BF), below.astype(BF)]
    for sub in range(2):
        west, east = choose(az_even, az_b[sub], az_a[sub]), choose(az_even, az_a[sub], az_b[sub])
        near_term = dot(jnp.concatenate([along[sub], west, east], axis=1), near_weights[sub])
        solved[sub] = jnp.where(keep[sub] > 0.0, base[sub] - near_term, 0.0)


def far_in_kernel(received, solved, far_weights, out):
    rhs_count = solved.shape[1]
    rank = far_weights.shape[0] // 2
    sums = jnp.sum(received[...].astype(F32), axis=0)
    chunks = sums.shape[0] // 2
    lanes = sums.shape[1]
    own = iota((rhs_count, lanes), 1) % rhs_count == iota((rhs_count, lanes), 0)
    spaced = [jnp.where(own, sums[row : row + 1], 0.0).astype(BF) for row in range(2 * chunks)]
    spaced = [jnp.concatenate(spaced[sub * chunks : (sub + 1) * chunks], axis=1) for sub in range(2)]
    size = (chunks * lanes, 2 * rank)
    select = (iota(size, 0) // rhs_count == iota(size, 1) % rank).astype(BF)
    far_in = dot(jnp.concatenate(spaced, axis=0), select)
    block = iota(far_in.shape, 0) // rhs_count == iota(far_in.shape, 1) // rank
    far_term = dot(jnp.where(block, far_in, 0.0).astype(BF), far_weights[...])
    for sub in range(2):
        out[sub] = solved[sub] - far_term[sub * rhs_count : (sub + 1) * rhs_count]


def swap(value, axis, start):
    sec_count, az_count = lax.axis_size("sec"), 2 * lax.axis_size("y")
    route = []
    for sec in range(sec_count):
        for az in range(az_count):
            if axis == "az":
                step = 1 if (az - start) % 2 == 0 else -1
                to = sec, (az + step) % az_count
            else:
                step = 1 if (sec - start) % 2 == 0 else -1
                to = (sec + step, az) if 0 <= sec + step < sec_count else (sec, az ^ 1)
            route.append((sec * az_count + az, to[0] * az_count + to[1]))
    return lax.ppermute(value, ALL, route)


def in_hbm(array):
    return pltpu.with_memory_space_constraint(array, pltpu.HBM)


def call(kernel, out_shape, in_specs, flops, moved, grant, scratch=(), out_specs=None):
    return pl.pallas_call(
        kernel,
        out_shape=out_shape,
        in_specs=in_specs,
        out_specs=out_specs or jax.tree.map(lambda _: VMEM, out_shape),
        scratch_shapes=scratch,
        compiler_params=pltpu.CompilerParams(vmem_limit_bytes=grant * MIB),
        cost_estimate=pl.CostEstimate(flops=flops, bytes_accessed=moved, transcendentals=0),
    )


def shape(dims, dtype=BF):
    return jax.ShapeDtypeStruct(dims, dtype)


def local(
    currents,
    right_side,
    counts,
    inverse_blocks,
    near_out,
    near_in,
    far_source_basis,
    far_target_basis,
    far_cores,
    far_target_device,
    far_target_half,
    far_source_half,
):
    _, rhs_count, row_count = currents.shape
    far_rank = far_source_basis.shape[1]
    near_rank = near_out.shape[2]
    far_len = far_cores.shape[0]
    sec_count = lax.axis_size("sec")
    az_count = 2 * lax.axis_size("y")
    devices = sec_count * az_count
    width = 256
    chunks = far_cores.shape[1] // width
    lanes = width // far_rank * rhs_count

    piece = shape((rhs_count, near_rank))
    pair = shape((2, rhs_count, near_rank))
    steps = 3
    fetched = [counts, currents, far_source_basis, far_target_device.reshape(1, far_len), far_target_half, far_source_half]
    packed, sec_a, sec_b, az_a, az_b, kept, keep = call(
        send_kernel,
        (
            shape((devices, 2 * chunks, lanes)),
            piece,
            piece,
            pair,
            pair,
            pair,
            shape((2, 1, row_count), F32),
        ),
        [HBM] * 8,
        2 * 2 * devices * far_len * row_count,
        2 * far_cores.size,
        20,
        [
            pltpu.SMEM(counts.shape, jnp.int32),
            pltpu.VMEM(currents.shape, F32),
            pltpu.VMEM(far_source_basis.shape, BF),
            pltpu.VMEM((1, far_len), jnp.int32),
            pltpu.VMEM((far_len,), jnp.int32),
            pltpu.VMEM((far_len,), jnp.int32),
            pltpu.VMEM((steps, far_len // steps, far_cores.shape[1]), BF),
            pltpu.VMEM(near_out.shape, BF),
            pltpu.VMEM((far_len, chunks * lanes), BF),
            pltpu.VMEM((2 * devices * chunks + 8, lanes), F32),
            pltpu.VMEM((devices, 2 * chunks, lanes), BF),
            pltpu.VMEM(currents.shape, BF),
            pltpu.SemaphoreType.DMA((8 + steps,)),
        ],
        (HBM,) + (VMEM,) * 6,
    )(*[in_hbm(x) for x in fetched + [far_cores, near_out]])
    received = lax.all_to_all(packed, ("core", "sec", "y"), split_axis=0, concat_axis=0, tiled=True)
    sec_a, sec_b = swap(sec_a, "sec", 0), swap(sec_b, "sec", 1)
    az_a, az_b = swap(az_a, "az", 0), swap(az_b, "az", 1)

    parts = 1
    base, near_weights, far_weights = call(
        solve_kernel,
        (
            shape((2, rhs_count, row_count), F32),
            shape((2, 3 * near_rank, row_count)),
            shape((2 * far_rank, row_count)),
        ),
        [VMEM] * 2 + [HBM] * 4,
        2 * inverse_blocks.size * (3 * near_rank + 2 * rhs_count + far_rank),
        inverse_blocks.size * 2,
        16,
        [
            pltpu.VMEM(right_side.shape, F32),
            pltpu.VMEM(far_target_basis.shape, BF),
            pltpu.VMEM(near_in.shape, BF),
            pltpu.VMEM((2, parts, row_count // parts, row_count), BF),
            pltpu.SemaphoreType.DMA((4 + 2 * parts,)),
        ],
    )(keep, kept, *[in_hbm(x) for x in [right_side, far_target_basis, near_in, inverse_blocks]])

    solved = call(
        near_in_kernel,
        shape(right_side.shape, F32),
        [VMEM] * 7,
        2 * 2 * rhs_count * 3 * near_rank * row_count,
        2 * near_in.size,
        4,
    )(keep, sec_a, sec_b, az_a, az_b, base, near_weights)

    return call(
        far_in_kernel,
        shape(right_side.shape, F32),
        [VMEM] * 3,
        2 * 2 * rhs_count * far_rank * row_count,
        received.size * 2,
        4,
    )(received, solved, far_weights)


def solution(mesh):
    sec_count, az_count = mesh.devices.shape
    inner = jax.sharding.Mesh(mesh.devices.reshape(sec_count, az_count // 2, 2), ALL)
    in_specs = (P(ALL),) * 12
    return jax.shard_map(local, mesh=inner, in_specs=in_specs, out_specs=P(ALL), check_vma=False)
```

```python
import jax
import jax.numpy as jnp
from jax import lax
from jax.experimental import pallas as pl
from jax.experimental.pallas import tpu as pltpu
from jax.sharding import PartitionSpec as P

BF = jnp.bfloat16
F32 = jnp.float32
VMEM = pl.BlockSpec(memory_space=pltpu.VMEM)
HBM = pl.BlockSpec(memory_space=pltpu.HBM)
MIB = 1024 * 1024
NT = (((1,), (1,)), ((), ()))
ALL = ("sec", "y", "core")


def iota(shape, dim):
    return lax.broadcasted_iota(jnp.int32, shape, dim)


def dot(a, b, dims=(((1,), (0,)), ((), ()))):
    return lax.dot_general(a, b, dims, preferred_element_type=F32)


def send_kernel(
    counts_hbm, currents_hbm, basis_hbm, device_hbm, target_hbm, source_hbm, cores_hbm, near_hbm,
    packed_hbm, sec_a, sec_b, az_a, az_b, kept, keep,
    counts, currents, basis, device, target_half, source_half, cores, near, terms, staged, packed, masked, sems,
):
    steps, rows = cores.shape[:2]
    pairs = [
        (counts_hbm, counts),
        (currents_hbm, currents),
        (basis_hbm, basis),
        (device_hbm, device),
        (target_hbm, target_half),
        (source_hbm, source_half),
    ]
    pairs += [(cores_hbm.at[pl.ds(step * rows, rows)], cores.at[step]) for step in range(steps)]
    pairs += [(near_hbm, near)]
    copies = [pltpu.make_async_copy(source, to, sems.at[i]) for i, (source, to) in enumerate(pairs)]
    for copy in copies:
        copy.start()
    for copy in copies[:6]:
        copy.wait()

    chunks = packed.shape[1] // 2
    lanes = packed.shape[2]
    rhs_count = currents.shape[1]
    far_rank = basis.shape[1]
    width = cores.shape[2] // chunks
    targets = 2 * packed.shape[0]

    for sub in range(2):
        keep[sub] = (iota(keep.shape[1:], 1) < counts[sub]).astype(F32)
        masked[sub] = jnp.where(iota(currents.shape[1:], 1) < counts[sub], currents[sub], 0.0).astype(BF)
    both_masked = jnp.concatenate([masked[0], masked[1]], axis=0)
    projected = [dot(basis[sub], both_masked, NT).astype(BF) for sub in range(2)]
    size = (2 * rhs_count, 2 * lanes)
    repeat = iota(size, 1) // lanes * rhs_count + iota(size, 1) % rhs_count == iota(size, 0)
    repeat = repeat.astype(BF)
    size = (width, 2 * lanes)
    diagonal = iota(size, 0) // far_rank == iota(size, 1) % lanes // rhs_count
    tiled = [dot(projected[sub], repeat)[:, sub * lanes : (sub + 1) * lanes] for sub in range(2)]
    tiled = jnp.concatenate([jnp.concatenate(tiled, axis=1)] * (width // far_rank), axis=0)
    spread = jnp.where(diagonal, tiled, 0.0).astype(BF)

    source = source_half[...].reshape(device.shape).astype(F32)
    count = device.shape[1]
    second = [
        jnp.broadcast_to(source[:, start : start + lanes], (lanes, lanes)).T > 0.5 for start in range(0, count, lanes)
    ]
    place = device[...] % 2 * (targets // 4) + device[...] // 2
    target = place * 2 + target_half[...].reshape(device.shape)
    onehot = (iota((targets, count), 0) == target).astype(BF)

    sums = None
    for step in range(steps + 1):
        if step < steps:
            copies[6 + step].wait()
            for k in range(chunks):
                both = dot(cores[step, :, k * width : (k + 1) * width], spread)
                for part in range(rows // lanes):
                    piece = both[part * lanes : (part + 1) * lanes]
                    chosen = jnp.where(second[step * (rows // lanes) + part], piece[:, lanes:], piece[:, :lanes])
                    terms[pl.ds(step * rows + part * lanes, lanes), pl.ds(k * lanes, lanes)] = chosen.astype(BF)
        if step > 0:
            part = slice((step - 1) * rows, step * rows)
            term = dot(onehot[:, part], terms[part, :])
            sums = term if sums is None else sums + term
    for k in range(chunks):
        staged[pl.ds(k, targets, stride=chunks), :] = sums[:, k * lanes : (k + 1) * lanes]
    packed[...] = staged[: targets * chunks, :].reshape(packed.shape).astype(BF)
    sent = pltpu.make_async_copy(packed, packed_hbm, sems.at[7 + steps])
    sent.start()

    copies[6 + steps].wait()
    rank = sec_a.shape[1]
    sec_even, az_even = even("sec"), even("az")
    coeffs = []
    for sub in range(2):
        coeffs.append(dot(masked[sub], near[sub].reshape(4 * rank, near.shape[3]), NT))
    kept[0] = coeffs[0][:, :rank].astype(BF)
    kept[1] = coeffs[1][:, rank : 2 * rank].astype(BF)
    to_next, to_previous = coeffs[1][:, :rank], coeffs[0][:, rank : 2 * rank]
    sec_a[...] = choose(sec_even, to_next, to_previous)
    sec_b[...] = choose(sec_even, to_previous, to_next)
    for sub in range(2):
        to_next, to_previous = coeffs[sub][:, 2 * rank : 3 * rank], coeffs[sub][:, 3 * rank :]
        az_a[sub] = choose(az_even, to_next, to_previous)
        az_b[sub] = choose(az_even, to_previous, to_next)
    sent.wait()


def even(axis):
    return lax.axis_index("core") == 0 if axis == "az" else lax.rem(lax.axis_index(axis), 2) == 0


def choose(first, yes, no):
    return jnp.where(first, yes.astype(F32), no.astype(F32)).astype(BF)


def solve_kernel(
    keep, kept, right_hbm, basis_hbm, near_hbm, inverse_hbm,
    base, near_weights, far_weights,
    right_side, basis, near_in, inverse, sems,
):
    parts, rows = inverse.shape[1:3]
    pairs = [(right_hbm, right_side), (basis_hbm, basis)]
    for sub in range(2):
        pairs.append((near_hbm.at[sub], near_in.at[sub]))
        pairs += [(inverse_hbm.at[sub, pl.ds(part * rows, rows)], inverse.at[sub, part]) for part in range(parts)]
    copies = [pltpu.make_async_copy(source, to, sems.at[i]) for i, (source, to) in enumerate(pairs)]
    for copy in copies:
        copy.start()
    for copy in copies[:2]:
        copy.wait()
    rhs_count = right_side.shape[1]
    far_rank = basis.shape[1]
    near_rows = near_weights.shape[1]
    for sub in range(2):
        own = copies[2 + sub * (parts + 1) :]
        own[0].wait()
        rest = jnp.where(keep[sub] > 0.0, right_side[sub], 0.0) - dot(kept[1 - sub], near_in[sub, 1 - sub])
        high = rest.astype(BF)
        low = (rest - high.astype(F32)).astype(BF)
        factors = [near_in[sub, sub], near_in[sub, 2], near_in[sub, 3]]
        stacked = jnp.concatenate(factors + [high, low, basis[sub]], axis=0)
        for part in range(parts):
            own[1 + part].wait()
            solved = dot(stacked, inverse[sub, part], NT)
            columns = pl.ds(part * rows, rows)
            near_weights[sub, :, columns] = solved[:near_rows].astype(BF)
            rest = solved[near_rows:]
            base[sub, :, columns] = rest[:rhs_count] + rest[rhs_count : 2 * rhs_count]
            rest = jnp.where(keep[sub, :, part * rows : (part + 1) * rows] > 0.0, rest[2 * rhs_count :], 0.0)
            far_weights[pl.ds(sub * far_rank, far_rank), columns] = rest.astype(BF)


def near_in_kernel(keep, sec_a, sec_b, az_a, az_b, base, near_weights, solved, select, block):
    rhs_count = base.shape[1]
    rank = select.shape[1] // 2
    select[...] = (iota(select.shape, 0) // rhs_count == iota(select.shape, 1) % rank).astype(BF)
    block[...] = (iota(block.shape, 0) // rhs_count == iota(block.shape, 1) // rank).astype(F32)
    sec_even, az_even = even("sec"), even("az")
    section = lax.axis_index("sec")
    above = jnp.where(section == 0, 0.0, choose(sec_even, sec_b[...], sec_a[...]).astype(F32))
    below = jnp.where(section == lax.axis_size("sec") - 1, 0.0, choose(sec_even, sec_a[...], sec_b[...]).astype(F32))
    along = [above.astype(BF), below.astype(BF)]
    for sub in range(2):
        west, east = choose(az_even, az_b[sub], az_a[sub]), choose(az_even, az_a[sub], az_b[sub])
        near_term = dot(jnp.concatenate([along[sub], west, east], axis=1), near_weights[sub])
        solved[sub] = jnp.where(keep[sub] > 0.0, base[sub] - near_term, 0.0)


def far_in_kernel(received, solved, far_weights, select, block, out):
    rhs_count = solved.shape[1]
    sums = jnp.sum(received[...].astype(F32), axis=0)
    chunks = sums.shape[0] // 2
    lanes = sums.shape[1]
    own = iota((rhs_count, lanes), 1) % rhs_count == iota((rhs_count, lanes), 0)
    spaced = [jnp.where(own, sums[row : row + 1], 0.0).astype(BF) for row in range(2 * chunks)]
    spaced = [jnp.concatenate(spaced[sub * chunks : (sub + 1) * chunks], axis=1) for sub in range(2)]
    far_in = dot(jnp.concatenate(spaced, axis=0), select[...])
    far_term = dot((far_in * block[...]).astype(BF), far_weights[...])
    for sub in range(2):
        out[sub] = solved[sub] - far_term[sub * rhs_count : (sub + 1) * rhs_count]


def swap(value, axis, start):
    sec_count, az_count = lax.axis_size("sec"), 2 * lax.axis_size("y")
    route = []
    for sec in range(sec_count):
        for az in range(az_count):
            if axis == "az":
                step = 1 if (az - start) % 2 == 0 else -1
                to = sec, (az + step) % az_count
            else:
                step = 1 if (sec - start) % 2 == 0 else -1
                to = (sec + step, az) if 0 <= sec + step < sec_count else (sec, az ^ 1)
            route.append((sec * az_count + az, to[0] * az_count + to[1]))
    return lax.ppermute(value, ALL, route)


def in_hbm(array):
    return pltpu.with_memory_space_constraint(array, pltpu.HBM)


def call(kernel, out_shape, in_specs, flops, moved, grant, scratch=(), out_specs=None):
    return pl.pallas_call(
        kernel,
        out_shape=out_shape,
        in_specs=in_specs,
        out_specs=out_specs or jax.tree.map(lambda _: VMEM, out_shape),
        scratch_shapes=scratch,
        compiler_params=pltpu.CompilerParams(vmem_limit_bytes=grant * MIB),
        cost_estimate=pl.CostEstimate(flops=flops, bytes_accessed=moved, transcendentals=0),
    )


def shape(dims, dtype=BF):
    return jax.ShapeDtypeStruct(dims, dtype)


def local(
    currents,
    right_side,
    counts,
    inverse_blocks,
    near_out,
    near_in,
    far_source_basis,
    far_target_basis,
    far_cores,
    far_target_device,
    far_target_half,
    far_source_half,
):
    _, rhs_count, row_count = currents.shape
    far_rank = far_source_basis.shape[1]
    near_rank = near_out.shape[2]
    far_len = far_cores.shape[0]
    sec_count = lax.axis_size("sec")
    az_count = 2 * lax.axis_size("y")
    devices = sec_count * az_count
    width = 256
    chunks = far_cores.shape[1] // width
    lanes = width // far_rank * rhs_count

    piece = shape((rhs_count, near_rank))
    pair = shape((2, rhs_count, near_rank))
    steps = 3
    fetched = [counts, currents, far_source_basis, far_target_device.reshape(1, far_len), far_target_half, far_source_half]
    packed, sec_a, sec_b, az_a, az_b, kept, keep = call(
        send_kernel,
        (
            shape((devices, 2 * chunks, lanes)),
            piece,
            piece,
            pair,
            pair,
            pair,
            shape((2, 1, row_count), F32),
        ),
        [HBM] * 8,
        2 * 2 * devices * far_len * row_count,
        2 * far_cores.size,
        20,
        [
            pltpu.SMEM(counts.shape, jnp.int32),
            pltpu.VMEM(currents.shape, F32),
            pltpu.VMEM(far_source_basis.shape, BF),
            pltpu.VMEM((1, far_len), jnp.int32),
            pltpu.VMEM((far_len,), jnp.int32),
            pltpu.VMEM((far_len,), jnp.int32),
            pltpu.VMEM((steps, far_len // steps, far_cores.shape[1]), BF),
            pltpu.VMEM(near_out.shape, BF),
            pltpu.VMEM((far_len, chunks * lanes), BF),
            pltpu.VMEM((2 * devices * chunks + 8, lanes), F32),
            pltpu.VMEM((devices, 2 * chunks, lanes), BF),
            pltpu.VMEM(currents.shape, BF),
            pltpu.SemaphoreType.DMA((8 + steps,)),
        ],
        (HBM,) + (VMEM,) * 6,
    )(*[in_hbm(x) for x in fetched + [far_cores, near_out]])
    received = lax.all_to_all(packed, ("core", "sec", "y"), split_axis=0, concat_axis=0, tiled=True)
    sec_a, sec_b = swap(sec_a, "sec", 0), swap(sec_b, "sec", 1)
    az_a, az_b = swap(az_a, "az", 0), swap(az_b, "az", 1)

    parts = 1
    base, near_weights, far_weights = call(
        solve_kernel,
        (
            shape((2, rhs_count, row_count), F32),
            shape((2, 3 * near_rank, row_count)),
            shape((2 * far_rank, row_count)),
        ),
        [VMEM] * 2 + [HBM] * 4,
        2 * inverse_blocks.size * (3 * near_rank + 2 * rhs_count + far_rank),
        inverse_blocks.size * 2,
        16,
        [
            pltpu.VMEM(right_side.shape, F32),
            pltpu.VMEM(far_target_basis.shape, BF),
            pltpu.VMEM(near_in.shape, BF),
            pltpu.VMEM((2, parts, row_count // parts, row_count), BF),
            pltpu.SemaphoreType.DMA((4 + 2 * parts,)),
        ],
    )(keep, kept, *[in_hbm(x) for x in [right_side, far_target_basis, near_in, inverse_blocks]])

    solved, select, block = call(
        near_in_kernel,
        (
            shape(right_side.shape, F32),
            shape((chunks * lanes, 2 * far_rank)),
            shape((2 * rhs_count, 2 * far_rank), F32),
        ),
        [VMEM] * 7,
        2 * 2 * rhs_count * 3 * near_rank * row_count,
        2 * near_in.size,
        4,
    )(keep, sec_a, sec_b, az_a, az_b, base, near_weights)

    return call(
        far_in_kernel,
        shape(right_side.shape, F32),
        [VMEM] * 5,
        2 * 2 * rhs_count * far_rank * row_count,
        received.size * 2,
        4,
    )(received, solved, far_weights, select, block)


def solution(mesh):
    sec_count, az_count = mesh.devices.shape
    inner = jax.sharding.Mesh(mesh.devices.reshape(sec_count, az_count // 2, 2), ALL)
    in_specs = (P(ALL),) * 12
    return jax.shard_map(local, mesh=inner, in_specs=in_specs, out_specs=P(ALL), check_vma=False)
```

```python
import jax
import jax.numpy as jnp
from jax import lax
from jax.experimental import pallas as pl
from jax.experimental.pallas import tpu as pltpu
from jax.sharding import PartitionSpec as P

BF = jnp.bfloat16
F32 = jnp.float32
VMEM = pl.BlockSpec(memory_space=pltpu.VMEM)
HBM = pl.BlockSpec(memory_space=pltpu.HBM)
MIB = 1024 * 1024
NT = (((1,), (1,)), ((), ()))
ALL = ("sec", "y", "core")


def iota(shape, dim):
    return lax.broadcasted_iota(jnp.int32, shape, dim)


def dot(a, b, dims=(((1,), (0,)), ((), ()))):
    return lax.dot_general(a, b, dims, preferred_element_type=F32)


def send_kernel(
    counts_hbm, currents_hbm, basis_hbm, device_hbm, target_hbm, source_hbm, cores_hbm, near_hbm,
    packed_hbm, sec_a, sec_b, az_a, az_b, kept, keep,
    counts, currents, basis, device, target_half, source_half, cores, near, terms, staged, packed, masked, sems,
):
    steps, rows = cores.shape[:2]
    pairs = [
        (counts_hbm, counts),
        (currents_hbm, currents),
        (basis_hbm, basis),
        (device_hbm, device),
        (target_hbm, target_half),
        (source_hbm, source_half),
    ]
    pairs += [(cores_hbm.at[pl.ds(step * rows, rows)], cores.at[step]) for step in range(steps)]
    pairs += [(near_hbm, near)]
    copies = [pltpu.make_async_copy(source, to, sems.at[i]) for i, (source, to) in enumerate(pairs)]
    for copy in copies:
        copy.start()
    for copy in copies[:6]:
        copy.wait()

    chunks = packed.shape[1] // 2
    lanes = packed.shape[2]
    rhs_count = currents.shape[1]
    far_rank = basis.shape[1]
    width = cores.shape[2] // chunks
    targets = 2 * packed.shape[0]

    for sub in range(2):
        keep[sub] = (iota(keep.shape[1:], 1) < counts[sub]).astype(F32)
        masked[sub] = jnp.where(iota(currents.shape[1:], 1) < counts[sub], currents[sub], 0.0).astype(BF)
    both_masked = jnp.concatenate([masked[0], masked[1]], axis=0)
    projected = [dot(basis[sub], both_masked, NT).astype(BF) for sub in range(2)]
    size = (2 * rhs_count, 2 * lanes)
    repeat = iota(size, 1) // lanes * rhs_count + iota(size, 1) % rhs_count == iota(size, 0)
    repeat = repeat.astype(BF)
    size = (width, 2 * lanes)
    diagonal = iota(size, 0) // far_rank == iota(size, 1) % lanes // rhs_count
    tiled = [dot(projected[sub], repeat)[:, sub * lanes : (sub + 1) * lanes] for sub in range(2)]
    tiled = jnp.concatenate([jnp.concatenate(tiled, axis=1)] * (width // far_rank), axis=0)
    spread = jnp.where(diagonal, tiled, 0.0).astype(BF)

    source = source_half[...].reshape(device.shape).astype(F32)
    count = device.shape[1]
    second = [
        jnp.broadcast_to(source[:, start : start + lanes], (lanes, lanes)).T > 0.5 for start in range(0, count, lanes)
    ]
    place = device[...] % 2 * (targets // 4) + device[...] // 2
    target = place * 2 + target_half[...].reshape(device.shape)
    onehot = (iota((targets, count), 0) == target).astype(BF)

    sums = None
    for step in range(steps + 1):
        if step < steps:
            copies[6 + step].wait()
            for k in range(chunks):
                both = dot(cores[step, :, k * width : (k + 1) * width], spread)
                for part in range(rows // lanes):
                    piece = both[part * lanes : (part + 1) * lanes]
                    chosen = jnp.where(second[step * (rows // lanes) + part], piece[:, lanes:], piece[:, :lanes])
                    terms[pl.ds(step * rows + part * lanes, lanes), pl.ds(k * lanes, lanes)] = chosen.astype(BF)
        if step > 0:
            part = slice((step - 1) * rows, step * rows)
            term = dot(onehot[:, part], terms[part, :])
            sums = term if sums is None else sums + term
    halves = []
    for half in range(2):
        some = targets // 2
        for k in range(chunks):
            piece = sums[half * some : (half + 1) * some, k * lanes : (k + 1) * lanes]
            staged[pl.ds(half * some * chunks + k, some, stride=chunks), :] = piece
        part = pl.ds(half * some // 2, some // 2)
        piece = staged[pl.ds(half * some * chunks, some * chunks), :]
        packed[part] = piece.reshape(some // 2, 2 * chunks, lanes).astype(BF)
        halves.append(pltpu.make_async_copy(packed.at[part], packed_hbm.at[part], sems.at[7 + steps + half]))
        halves[-1].start()

    copies[6 + steps].wait()
    rank = sec_a.shape[1]
    sec_even, az_even = even("sec"), even("az")
    coeffs = []
    for sub in range(2):
        coeffs.append(dot(masked[sub], near[sub].reshape(4 * rank, near.shape[3]), NT))
    kept[0] = coeffs[0][:, :rank].astype(BF)
    kept[1] = coeffs[1][:, rank : 2 * rank].astype(BF)
    to_next, to_previous = coeffs[1][:, :rank], coeffs[0][:, rank : 2 * rank]
    sec_a[...] = choose(sec_even, to_next, to_previous)
    sec_b[...] = choose(sec_even, to_previous, to_next)
    for sub in range(2):
        to_next, to_previous = coeffs[sub][:, 2 * rank : 3 * rank], coeffs[sub][:, 3 * rank :]
        az_a[sub] = choose(az_even, to_next, to_previous)
        az_b[sub] = choose(az_even, to_previous, to_next)
    for copy in halves:
        copy.wait()


def even(axis):
    return lax.axis_index("core") == 0 if axis == "az" else lax.rem(lax.axis_index(axis), 2) == 0


def choose(first, yes, no):
    return jnp.where(first, yes.astype(F32), no.astype(F32)).astype(BF)


def solve_kernel(
    keep, kept, right_hbm, basis_hbm, near_hbm, inverse_hbm,
    base, near_weights, far_weights,
    right_side, basis, near_in, inverse, sems,
):
    parts, rows = inverse.shape[1:3]
    pairs = [(right_hbm, right_side), (basis_hbm, basis)]
    for sub in range(2):
        pairs.append((near_hbm.at[sub], near_in.at[sub]))
        pairs += [(inverse_hbm.at[sub, pl.ds(part * rows, rows)], inverse.at[sub, part]) for part in range(parts)]
    copies = [pltpu.make_async_copy(source, to, sems.at[i]) for i, (source, to) in enumerate(pairs)]
    for copy in copies:
        copy.start()
    for copy in copies[:2]:
        copy.wait()
    rhs_count = right_side.shape[1]
    far_rank = basis.shape[1]
    near_rows = near_weights.shape[1]
    for sub in range(2):
        own = copies[2 + sub * (parts + 1) :]
        own[0].wait()
        rest = jnp.where(keep[sub] > 0.0, right_side[sub], 0.0) - dot(kept[1 - sub], near_in[sub, 1 - sub])
        high = rest.astype(BF)
        low = (rest - high.astype(F32)).astype(BF)
        factors = [near_in[sub, sub], near_in[sub, 2], near_in[sub, 3]]
        stacked = jnp.concatenate(factors + [high, low, basis[sub]], axis=0)
        for part in range(parts):
            own[1 + part].wait()
            solved = dot(stacked, inverse[sub, part], NT)
            columns = pl.ds(part * rows, rows)
            near_weights[sub, :, columns] = solved[:near_rows].astype(BF)
            rest = solved[near_rows:]
            base[sub, :, columns] = rest[:rhs_count] + rest[rhs_count : 2 * rhs_count]
            rest = jnp.where(keep[sub, :, part * rows : (part + 1) * rows] > 0.0, rest[2 * rhs_count :], 0.0)
            far_weights[pl.ds(sub * far_rank, far_rank), columns] = rest.astype(BF)


def near_in_kernel(keep, sec_a, sec_b, az_a, az_b, base, near_weights, solved):
    sec_even, az_even = even("sec"), even("az")
    section = lax.axis_index("sec")
    above = jnp.where(section == 0, 0.0, choose(sec_even, sec_b[...], sec_a[...]).astype(F32))
    below = jnp.where(section == lax.axis_size("sec") - 1, 0.0, choose(sec_even, sec_a[...], sec_b[...]).astype(F32))
    along = [above.astype(BF), below.astype(BF)]
    for sub in range(2):
        west, east = choose(az_even, az_b[sub], az_a[sub]), choose(az_even, az_a[sub], az_b[sub])
        near_term = dot(jnp.concatenate([along[sub], west, east], axis=1), near_weights[sub])
        solved[sub] = jnp.where(keep[sub] > 0.0, base[sub] - near_term, 0.0)


def far_in_kernel(received, solved, far_weights, out):
    rhs_count = solved.shape[1]
    rank = far_weights.shape[0] // 2
    sums = jnp.sum(received[...].astype(F32), axis=0)
    chunks = sums.shape[0] // 2
    lanes = sums.shape[1]
    own = iota((rhs_count, lanes), 1) % rhs_count == iota((rhs_count, lanes), 0)
    spaced = [jnp.where(own, sums[row : row + 1], 0.0).astype(BF) for row in range(2 * chunks)]
    spaced = [jnp.concatenate(spaced[sub * chunks : (sub + 1) * chunks], axis=1) for sub in range(2)]
    size = (chunks * lanes, 2 * rank)
    select = (iota(size, 0) // rhs_count == iota(size, 1) % rank).astype(BF)
    far_in = dot(jnp.concatenate(spaced, axis=0), select)
    block = iota(far_in.shape, 0) // rhs_count == iota(far_in.shape, 1) // rank
    far_term = dot(jnp.where(block, far_in, 0.0).astype(BF), far_weights[...])
    for sub in range(2):
        out[sub] = solved[sub] - far_term[sub * rhs_count : (sub + 1) * rhs_count]


def swap(value, axis, start):
    sec_count, az_count = lax.axis_size("sec"), 2 * lax.axis_size("y")
    route = []
    for sec in range(sec_count):
        for az in range(az_count):
            if axis == "az":
                step = 1 if (az - start) % 2 == 0 else -1
                to = sec, (az + step) % az_count
            else:
                step = 1 if (sec - start) % 2 == 0 else -1
                to = (sec + step, az) if 0 <= sec + step < sec_count else (sec, az ^ 1)
            route.append((sec * az_count + az, to[0] * az_count + to[1]))
    return lax.ppermute(value, ALL, route)


def in_hbm(array):
    return pltpu.with_memory_space_constraint(array, pltpu.HBM)


def call(kernel, out_shape, in_specs, flops, moved, grant, scratch=(), out_specs=None):
    return pl.pallas_call(
        kernel,
        out_shape=out_shape,
        in_specs=in_specs,
        out_specs=out_specs or jax.tree.map(lambda _: VMEM, out_shape),
        scratch_shapes=scratch,
        compiler_params=pltpu.CompilerParams(vmem_limit_bytes=grant * MIB),
        cost_estimate=pl.CostEstimate(flops=flops, bytes_accessed=moved, transcendentals=0),
    )


def shape(dims, dtype=BF):
    return jax.ShapeDtypeStruct(dims, dtype)


def local(
    currents,
    right_side,
    counts,
    inverse_blocks,
    near_out,
    near_in,
    far_source_basis,
    far_target_basis,
    far_cores,
    far_target_device,
    far_target_half,
    far_source_half,
):
    _, rhs_count, row_count = currents.shape
    far_rank = far_source_basis.shape[1]
    near_rank = near_out.shape[2]
    far_len = far_cores.shape[0]
    sec_count = lax.axis_size("sec")
    az_count = 2 * lax.axis_size("y")
    devices = sec_count * az_count
    width = 256
    chunks = far_cores.shape[1] // width
    lanes = width // far_rank * rhs_count

    piece = shape((rhs_count, near_rank))
    pair = shape((2, rhs_count, near_rank))
    steps = 3
    fetched = [counts, currents, far_source_basis, far_target_device.reshape(1, far_len), far_target_half, far_source_half]
    packed, sec_a, sec_b, az_a, az_b, kept, keep = call(
        send_kernel,
        (
            shape((devices, 2 * chunks, lanes)),
            piece,
            piece,
            pair,
            pair,
            pair,
            shape((2, 1, row_count), F32),
        ),
        [HBM] * 8,
        2 * 2 * devices * far_len * row_count,
        2 * far_cores.size,
        20,
        [
            pltpu.SMEM(counts.shape, jnp.int32),
            pltpu.VMEM(currents.shape, F32),
            pltpu.VMEM(far_source_basis.shape, BF),
            pltpu.VMEM((1, far_len), jnp.int32),
            pltpu.VMEM((far_len,), jnp.int32),
            pltpu.VMEM((far_len,), jnp.int32),
            pltpu.VMEM((steps, far_len // steps, far_cores.shape[1]), BF),
            pltpu.VMEM(near_out.shape, BF),
            pltpu.VMEM((far_len, chunks * lanes), BF),
            pltpu.VMEM((2 * devices * chunks + 8, lanes), F32),
            pltpu.VMEM((devices, 2 * chunks, lanes), BF),
            pltpu.VMEM(currents.shape, BF),
            pltpu.SemaphoreType.DMA((9 + steps,)),
        ],
        (HBM,) + (VMEM,) * 6,
    )(*[in_hbm(x) for x in fetched + [far_cores, near_out]])
    received = lax.all_to_all(packed, ("core", "sec", "y"), split_axis=0, concat_axis=0, tiled=True)
    sec_a, sec_b = swap(sec_a, "sec", 0), swap(sec_b, "sec", 1)
    az_a, az_b = swap(az_a, "az", 0), swap(az_b, "az", 1)

    parts = 1
    base, near_weights, far_weights = call(
        solve_kernel,
        (
            shape((2, rhs_count, row_count), F32),
            shape((2, 3 * near_rank, row_count)),
            shape((2 * far_rank, row_count)),
        ),
        [VMEM] * 2 + [HBM] * 4,
        2 * inverse_blocks.size * (3 * near_rank + 2 * rhs_count + far_rank),
        inverse_blocks.size * 2,
        16,
        [
            pltpu.VMEM(right_side.shape, F32),
            pltpu.VMEM(far_target_basis.shape, BF),
            pltpu.VMEM(near_in.shape, BF),
            pltpu.VMEM((2, parts, row_count // parts, row_count), BF),
            pltpu.SemaphoreType.DMA((4 + 2 * parts,)),
        ],
    )(keep, kept, *[in_hbm(x) for x in [right_side, far_target_basis, near_in, inverse_blocks]])

    solved = call(
        near_in_kernel,
        shape(right_side.shape, F32),
        [VMEM] * 7,
        2 * 2 * rhs_count * 3 * near_rank * row_count,
        2 * near_in.size,
        4,
    )(keep, sec_a, sec_b, az_a, az_b, base, near_weights)

    return call(
        far_in_kernel,
        shape(right_side.shape, F32),
        [VMEM] * 3,
        2 * 2 * rhs_count * far_rank * row_count,
        received.size * 2,
        4,
    )(received, solved, far_weights)


def solution(mesh):
    sec_count, az_count = mesh.devices.shape
    inner = jax.sharding.Mesh(mesh.devices.reshape(sec_count, az_count // 2, 2), ALL)
    in_specs = (P(ALL),) * 12
    return jax.shard_map(local, mesh=inner, in_specs=in_specs, out_specs=P(ALL), check_vma=False)
```
